32 devices in a mesh: dp: 4 (over z), pipe: 2 (over core), space: 4 (over y, x).
Axes of the slice: x: 2, y: 2, z: 4, core: 2. Of those that a mesh axis runs over, the one named last changes fastest.
Arguments:
- edges: bfloat16 [2, 8, 192, 384, 256], P('pipe', 'dp', 'space'), may hold values from -6 to 6
- mask_levels: int32 [192, 384, 256], P('space'), may hold values from 0 to 1, as said below
- norm_gains: float32 [2, 2, 256], P('pipe'), may hold values from 0.5 to 1.5
- norm_biases: float32 [2, 2, 256], P('pipe'), may hold values from -1.5 to 1.5
- filters: float32 [2, 2, 192, 256], P('pipe'), may hold values from -4 to 4
- w_in: bfloat16 [2, 256, 512], P('pipe'), may hold values from -0.375 to 0.375
- bias_in: float32 [2, 512], P('pipe'), may hold values from -1.5 to 1.5
- w_out: bfloat16 [2, 512, 256], P('pipe'), may hold values from -0.375 to 0.375
- bias_out: float32 [2, 256], P('pipe'), may hold values from -1.5 to 1.5
Outputs:
- ends: float32 [2, 8, 192, 384, 256], P('pipe', 'dp', 'space')
- grad_gains: float32 [2, 2, 256], P('pipe', None, 'space')
- grad_biases: float32 [2, 2, 256], P('pipe', None, 'space')
- grad_filters: float32 [2, 2, 192, 256], P('pipe', None, None, 'space')
- grad_w_in: float32 [2, 256, 512], P('pipe', 'space')
- grad_bias_in: float32 [2, 512], P('pipe', 'space')
- grad_w_out: float32 [2, 512, 256], P('pipe', 'space')
- grad_bias_out: float32 [2, 256], P('pipe', 'space')
The draws below stay inside these ranges and needn't reach their ends.
Inputs may be any that keep to these rules, and one draw needn't show every extreme that they name: `mask_levels`: each point has a ground level of 0 to 6, or 8; channel c of the point is live (1) exactly where c mod 8 is at least that level, so a point with level 8 has no live channel.
All inputs are finite; a program needn't handle non-finite values.
Results may differ from the reference program's by a relative error of at most 0.025.
Values may be sent and summed in bfloat16 or wider, within the bound.
A program may use at most 896 MiB of HBM per device.

```python
import math
import jax
import jax.numpy as jnp
from jax import lax

C = 256
FF = 512
NLAT = 192
NLON = 384
MODES = 192
BATCH = 8


def draw_mask_levels(key, part):
    key = jax.random.fold_in(key, 7)
    ground = jax.random.randint(key, (NLAT, NLON, 1), 0, 8)
    ground = jnp.where(ground == 7, 8, ground)
    channel_level = jnp.arange(C, dtype=jnp.int32) % 8
    return (channel_level[None, None, :] >= ground).astype(jnp.int32)


def block_levels(rng, dims, pieces, least, high):
    loudness = 1.0
    for axis_at, shards_of in pieces:
        draws = jax.random.uniform(jax.random.fold_in(jax.random.fold_in(rng, 6), axis_at), (shards_of,), jnp.float32, least / len(pieces), high / len(pieces))
        loudness = loudness * jnp.repeat(jnp.exp(draws), dims[axis_at] // shards_of).reshape((-1,) + (1,) * (len(dims) - 1 - axis_at))
    return loudness


def noise(key, extent, width, limit, pieces=(), kind=jnp.bfloat16):
    loudness = block_levels(key, extent, pieces, -0.22, 0.18) if pieces else 1.0
    entries = jax.random.normal(key, extent, jnp.float32) * width * loudness
    return jnp.minimum(jnp.maximum(entries, -limit), limit).astype(kind)


def setup_inputs(seed: int = 0) -> dict:
    keys = jax.random.split(jax.random.key(seed), 10)
    return {
        "edges": noise(keys[0], (2, BATCH, NLAT, NLON, C), 1.0, 6.0, ((0, 2), (1, 4), (2, 4))),
        "mask_levels": draw_mask_levels(jax.random.fold_in(keys[9], 71), 0),
        "norm_gains": jnp.clip(1.0 + 0.1 * jax.random.normal(keys[2], (2, 2, C), jnp.float32), 0.5, 1.5),
        "norm_biases": noise(keys[3], (2, 2, C), 0.3, 1.5, ((0, 2),), jnp.float32),
        "filters": noise(keys[4], (2, 2, NLAT, C), 0.7, 4.0, ((0, 2),), jnp.float32),
        "w_in": noise(keys[5], (2, C, FF), C ** -0.5, 0.375, ((0, 2),)),
        "bias_in": noise(keys[6], (2, FF), 0.3, 1.5, ((0, 2),), jnp.float32),
        "w_out": noise(keys[7], (2, FF, C), (FF // 2) ** -0.5, 0.375, ((0, 2),)),
        "bias_out": noise(keys[8], (2, C), 0.3, 1.5, ((0, 2),), jnp.float32),
    }


NORM_EPS = 1e-05
PRECISE = lax.Precision.HIGHEST

@jax.custom_vjp
def low(v):
    return lax.optimization_barrier(v.astype(jnp.bfloat16)).astype(jnp.float32)

@jax.custom_vjp
def low_back(v):
    return v

def low_keep(v):
    return (low(v), None)

def low_pass(kept, grad):
    return (grad,)

def back_keep(v):
    return (v, None)

def back_low(kept, grad):
    return (low(grad),)
low.defvjp(low_keep, low_pass)
low_back.defvjp(back_keep, back_low)

def legendre_table(orders, degree_count, colat_count):
    colatitude = (jnp.arange(colat_count, dtype=jnp.float32) + 0.5) * (math.pi / colat_count)
    cosine = jnp.cos(colatitude)
    sine_col = jnp.sin(colatitude)
    order_value = orders.astype(jnp.float32)[:, None]
    log_start = 0.5 * (jnp.log((2.0 * order_value + 1.0) / (4.0 * math.pi)) + lax.lgamma(order_value + 0.5) - lax.lgamma(order_value + 1.0) - 0.5 * math.log(math.pi)) + order_value * jnp.log(sine_col)[None, :]
    start_row = jnp.exp(log_start)

    def recurrence(pair_carry, degree):
        older_row, newer_row = pair_carry
        degree_value = degree.astype(jnp.float32)
        ahead_coef = jnp.sqrt(jnp.maximum(4.0 * degree_value * degree_value - 1.0, 0.0) / jnp.maximum(degree_value * degree_value - order_value * order_value, 1.0))
        degree_below = degree_value - 1.0
        behind = jnp.sqrt(jnp.maximum(degree_below * degree_below - order_value * order_value, 0.0) / jnp.maximum(4.0 * degree_below * degree_below - 1.0, 1.0))
        general = ahead_coef * (cosine * newer_row - behind * older_row)
        table_value = jnp.where(degree_value < order_value, 0.0, jnp.where(degree_value == order_value, start_row, general))
        return ((newer_row, table_value), table_value)
    zero_rows = jnp.zeros((orders.shape[0], colat_count), jnp.float32)
    last_pair, table_rows = lax.scan(recurrence, (zero_rows, zero_rows), jnp.arange(degree_count, dtype=jnp.int32))
    return (jnp.transpose(table_rows, (1, 0, 2)), sine_col)

def fourier_tables(order_count, lon_count):
    orders = jnp.arange(order_count, dtype=jnp.int32)
    points = jnp.arange(lon_count, dtype=jnp.int32)
    phase_index = orders[:, None] * points[None, :] % lon_count
    angle_value = phase_index.astype(jnp.float32) * (2.0 * math.pi / lon_count)
    dft_scale = 2.0 * math.pi / lon_count
    forward = jnp.stack([jnp.cos(angle_value) * dft_scale, -jnp.sin(angle_value) * dft_scale], axis=1).reshape(2 * order_count, lon_count)
    double = jnp.where(orders == 0, 1.0, 2.0).astype(jnp.float32)[:, None]
    inverse = jnp.stack([jnp.cos(angle_value) * double, -jnp.sin(angle_value) * double], axis=1).reshape(2 * order_count, lon_count)
    return (forward, jnp.transpose(inverse))

def norm_masked(values, live_mask, norm_gain, norm_bias):
    live_count = jnp.maximum(lax.optimization_barrier(jnp.sum(live_mask, axis=-1, keepdims=True)), 1.0)
    average = lax.optimization_barrier(jnp.sum(live_mask * values, axis=-1, keepdims=True)) / live_count
    centered = live_mask * (values - average)
    spread = lax.optimization_barrier(jnp.sum(centered * centered, axis=-1, keepdims=True)) / live_count
    return centered * lax.rsqrt(spread + NORM_EPS) * norm_gain + live_mask * norm_bias

def norm_plain(values, norm_gain, norm_bias):
    average = lax.optimization_barrier(jnp.mean(values, axis=-1, keepdims=True))
    centered = values - average
    spread = lax.optimization_barrier(jnp.mean(centered * centered, axis=-1, keepdims=True))
    return centered * lax.rsqrt(spread + NORM_EPS) * norm_gain + norm_bias

def filter_modes(coefficients, filter_real, filter_imag):
    real_part = coefficients[:, :, 0]
    imag_part = coefficients[:, :, 1]
    return jnp.stack([real_part * filter_real - imag_part * filter_imag, real_part * filter_imag + imag_part * filter_real], axis=2)

def apply_layer(values, live_mask, params, tables):
    gain_pair, bias_pair, filter_pair, weight_in, shift_in, weight_out, shift_out = params
    forward_dft, inverse_dft, analysis, synthesis = tables
    normed = low(norm_masked(values, live_mask, gain_pair[0], bias_pair[0]))
    spectrum = low(low_back(jnp.einsum('kw,hwc->hkc', forward_dft, normed, precision=PRECISE)))
    spectrum = spectrum.reshape(NLAT, MODES, 2, C)
    coefficients = low_back(jnp.einsum('mlh,hmrc->mlrc', analysis, spectrum, precision=PRECISE))
    filtered = low(filter_modes(coefficients, filter_pair[0], filter_pair[1]))
    synthesized = low(low_back(jnp.einsum('mlh,mlrc->hmrc', synthesis, filtered, precision=PRECISE)))
    mixed_grid = low_back(jnp.einsum('wk,hkc->hwc', inverse_dft, synthesized.reshape(NLAT, 2 * MODES, C), precision=PRECISE))
    residual = values + mixed_grid
    normed_two = low(norm_plain(residual, gain_pair[1], bias_pair[1])).reshape(NLAT * NLON, C)
    hidden = low_back(jnp.dot(normed_two, weight_in, precision=PRECISE)) + shift_in
    active = low(jax.nn.gelu(hidden, approximate=True))
    output = low_back(jnp.dot(active, weight_out, precision=PRECISE)) + shift_out
    return residual + output.reshape(NLAT, NLON, C)

def reference(edges, mask_levels, norm_gains, norm_biases, filters, w_in, bias_in, w_out, bias_out):
    forward_table, inverse_table = fourier_tables(MODES, NLON)
    legendre, sine_col = legendre_table(jnp.arange(MODES, dtype=jnp.int32), NLAT, NLAT)
    analysis = low(legendre * (sine_col * (math.pi / NLAT))[None, None, :])
    synthesis = low(legendre)
    tables = (low(forward_table), low(inverse_table), analysis, synthesis)
    live_mask = mask_levels.astype(jnp.float32)
    inputs = edges[0].astype(jnp.float32)
    cotangent = edges[1].astype(jnp.float32)
    weights = (norm_gains, norm_biases, filters, w_in.astype(jnp.float32), bias_in, w_out.astype(jnp.float32), bias_out)

    def network(inputs, weights):

        def per_sample(sample):
            for layer_number in range(2):
                sample = apply_layer(sample, live_mask, tuple((entry[layer_number] for entry in weights)), tables)
            return sample
        return lax.map(jax.checkpoint(per_sample), inputs)
    outputs, pullback = jax.vjp(network, inputs, weights)
    grad_inputs, weight_grads = pullback(cotangent)
    ends = jnp.stack([grad_inputs, outputs])
    return (ends,) + tuple(weight_grads)
```

```python
from collections import namedtuple
from functools import partial
import math

import jax
import jax.numpy as jnp
from jax import lax
from jax.experimental import pallas as pl
from jax.experimental.pallas import tpu as pltpu
from jax.sharding import PartitionSpec as P

NORM_EPS = 1e-05
BF = jnp.bfloat16
F32 = jnp.float32
MESH = pl.DeviceIdType.MESH
VMEM_BYTES = 58 * 2**20
TILE = 32
ROWS = 8
GELU_SCALE = math.sqrt(2.0 / math.pi)
GELU_CUBE = 0.044715

Dims = namedtuple(
    "Dims",
    ("bands", "lat", "lon", "ch", "own", "degrees", "ff", "rows", "chunks", "sub", "steps", "group",
     "low", "high"),
)


def matmul(a, b):
    return jnp.dot(a, b, preferred_element_type=F32)


def matmul_tn(a, b):
    return lax.dot_general(a, b, (((0,), (0,)), ((), ())), preferred_element_type=F32)


def matmul_nt(a, b):
    return lax.dot_general(a, b, (((1,), (1,)), ((), ())), preferred_element_type=F32)


def total(value):
    return jnp.sum(value, axis=-1, keepdims=True)


def folded(value):
    return jnp.sum(value.reshape(value.shape[0] // 8, 8, value.shape[1]), axis=0)


def dft_fill(table, inverse, by_order):
    orders, lon = table.shape[0] // 2, table.shape[0]
    order_axis = 0 if by_order else 1
    part = lax.broadcasted_iota(jnp.int32, table.shape, order_axis)
    imaginary = part >= orders
    order = jnp.where(imaginary, part - orders, part).astype(F32)
    point = lax.broadcasted_iota(jnp.int32, table.shape, 1 - order_axis).astype(F32)
    phase = order * point
    phase = phase - lon * jnp.floor(phase * (1.0 / lon))
    phase = jnp.where(phase >= lon, phase - lon, phase)
    angle = phase * (2.0 * math.pi / lon)
    value = jnp.where(imaginary, -jnp.sin(angle), jnp.cos(angle))
    scale = jnp.where(order == 0.0, 1.0, 2.0) if inverse else 2.0 * math.pi / lon
    table[...] = (value * scale).astype(BF)


def legendre_orders(orders):
    order_value = orders.astype(F32)
    factor = 0.5 * (
        jnp.log((2.0 * order_value + 1.0) / (4.0 * math.pi))
        + lax.lgamma(order_value + 0.5)
        - lax.lgamma(order_value + 1.0)
        - 0.5 * math.log(math.pi)
    )
    return jnp.stack([order_value, factor], axis=1)


def legendre_fill(first, orders, colat_count, first_lat, analysis, synthesis, rows):
    count, degrees, lat = analysis.shape
    own, width = orders.shape[0], -(-lat // 128) * 128
    order_value = jnp.broadcast_to(orders[:, 0:1], (own, width))
    square = order_value * order_value
    lats = jnp.minimum(lax.broadcasted_iota(jnp.int32, (8, width), 1) + first_lat, colat_count - 1)
    colatitude = (lats.astype(F32) + 0.5) * (math.pi / colat_count)
    sine = jnp.sin(colatitude)
    cosine = jnp.cos(colatitude)[0:1]
    weight = (sine * (math.pi / colat_count))[0:1]
    start = jnp.exp(orders[:, 1:2] + order_value * jnp.log(sine)[0:1])

    def recurrence(degree, pair):
        older, newer = pair
        value = (degree + first).astype(F32)
        ahead = jnp.sqrt(
            jnp.maximum(4.0 * value * value - 1.0, 0.0) / jnp.maximum(value * value - square, 1.0)
        )
        below = value - 1.0
        behind = jnp.sqrt(
            jnp.maximum(below * below - square, 0.0)
            / jnp.maximum(4.0 * below * below - 1.0, 1.0)
        )
        general = ahead * (cosine * newer - behind * older)
        row = jnp.where(value < order_value, 0.0, jnp.where(value == order_value, start, general))
        at = pl.multiple_of(degree * own, 8)
        for part in range(width // 128):
            rows[part, pl.ds(at, own), :] = row[:, part * 128 : (part + 1) * 128]
        return newer, row

    zero = start * 0.0
    lax.fori_loop(0, degrees, recurrence, (zero, zero))

    @pl.loop(0, count)
    def _(m):
        table = jnp.concatenate(
            [rows[part, pl.ds(m, degrees, stride=own), :] for part in range(width // 128)], axis=1
        )
        synthesis[m] = table[:, :lat].astype(BF)
        analysis[m] = (table * weight)[:, :lat].astype(BF)


def sides():
    me = lax.axis_index("space")
    return me + 1 - 2 * lax.rem(me, 2), lax.rem(me + 2, 4), 3 - me


def peers():
    core = lax.axis_index("pipe")
    x, y, across_both = sides()
    return [across_both, x + core * (y - x), y + core * (x - y)]


def greet(bands):
    barrier = pltpu.get_barrier_semaphore()
    for peer in peers():
        pl.semaphore_signal(barrier, inc=1, device_id={"space": peer}, device_id_type=MESH)


def await_peers(count):
    pl.semaphore_wait(pltpu.get_barrier_semaphore(), count)


def block_copies(bands, piece, source, place, sems, coming):
    out_sems, in_sems, own_sems = sems
    me = lax.axis_index("space")
    copies = []
    for turn, peer in enumerate(peers()):
        band = peer if coming else me
        copies.append(
            pltpu.make_async_remote_copy(
                src_ref=source(peer),
                dst_ref=place(band),
                send_sem=out_sems.at[piece, turn],
                recv_sem=in_sems.at[piece, turn],
                device_id={"space": peer},
                device_id_type=MESH,
            )
        )
    return copies


def own_copy(piece, source, place, sems):
    me = lax.axis_index("space")
    return pltpu.make_async_copy(source(me), place(me), sems[2].at[piece])


def start_piece(bands, piece, source, place, sems):
    for copy in block_copies(bands, piece, source, place, sems, False):
        copy.start()
    own_copy(piece, source, place, sems).start()


def finish_piece(bands, piece, source, place, sems):
    for copy in block_copies(bands, piece, source, place, sems, False):
        copy.wait_send()
    for copy in block_copies(bands, piece, source, place, sems, True):
        copy.wait_recv()
    own_copy(piece, source, place, sems).wait()


def side_copy(source, target, sems, slot, peer):
    return pltpu.make_async_remote_copy(
        src_ref=source,
        dst_ref=target,
        send_sem=sems[0].at[slot],
        recv_sem=sems[1].at[slot],
        device_id={"space": peer},
        device_id_type=MESH,
    )


def side_sems():
    return [pltpu.SemaphoreType.DMA((4,)), pltpu.SemaphoreType.DMA((4,)), pltpu.SemaphoreType.DMA((1,))]


def exchange_sems(bands, pieces):
    return [
        pltpu.SemaphoreType.DMA((pieces, bands - 1)),
        pltpu.SemaphoreType.DMA((pieces, bands - 1)),
        pltpu.SemaphoreType.DMA((pieces,)),
    ]


At = namedtuple("At", ("number", "chunk", "step", "last"))


def at_of(d, number):
    last = number == d.chunks * d.steps - 1
    return At(number, number // d.steps, lax.rem(number, d.steps), last)


def lat_stride(d):
    return 2 * d.bands * d.own + 8


def pack_rows(d, piece, wide, send):
    orders = d.bands * d.own
    for band in range(d.bands):

        @pl.loop(0, d.own, unroll=4)
        def _(m):
            for half in range(d.ch // 128):
                values = []
                for part in range(2):
                    at = part * orders + d.bands * m + band
                    values.append(wide[half, pl.ds(at, d.rows, stride=lat_stride(d)), :])
                lanes = slice(half * 128, half * 128 + 128)
                send[piece, band, m, :, lanes] = jnp.concatenate(values, axis=0).astype(BF)


def unpack_rows(d, block, wide):
    orders = d.bands * d.own
    for band in range(d.bands):

        @pl.loop(0, d.own, unroll=4)
        def _(m):
            value = block[band, m].astype(F32)
            for half in range(d.ch // 128):
                lanes = slice(half * 128, half * 128 + 128)
                for part in range(2):
                    at = part * orders + d.bands * m + band
                    wide[half, pl.ds(at, d.rows, stride=lat_stride(d)), :] = value[
                        part * d.rows : (part + 1) * d.rows, lanes
                    ]


def wide_rows(d, wide, k):
    orders = d.bands * d.own
    at = pl.multiple_of(k * lat_stride(d), 8)
    return jnp.concatenate(
        [wide[half, pl.ds(at, 2 * orders), :].astype(BF) for half in range(d.ch // 128)], axis=1
    )


def store_wide(d, wide, k, value):
    orders = d.bands * d.own
    at = pl.multiple_of(k * lat_stride(d), 8)
    for half in range(d.ch // 128):
        wide[half, pl.ds(at, 2 * orders), :] = value[:, half * 128 : (half + 1) * 128]


def modes_to_grid(d, at, table, wide, acc):
    for s in range(d.sub):
        k = at.step * d.sub + s
        acc[s * d.lon : (s + 1) * d.lon] = matmul(table[...], wide_rows(d, wide, k))


def grid_to_modes(d, at, table, low, wide):
    for s in range(d.sub):
        k = at.step * d.sub + s
        store_wide(d, wide, k, matmul(table[...], low[s * d.lon : (s + 1) * d.lon]))


def tiles(d):
    return [slice(t, t + TILE) for t in range(0, d.sub * d.lon, TILE)]


def spread(d, column):
    return jnp.broadcast_to(column, (TILE, 128))


def across(d, ref, t):
    return jnp.concatenate([ref[t].astype(F32)] * (d.ch // 128), axis=1)


def live_of(d, level, t):
    lane = lax.broadcasted_iota(jnp.int32, (TILE, d.ch), 1)
    return lax.rem(lane, 8).astype(F32) >= across(d, level, t)


def inverse_count(d, level, t):
    return 1.0 / jnp.maximum((d.ch // 8) * (8.0 - level[t].astype(F32)), 1.0)


def masked(live, value):
    return jnp.where(live, value, 0.0)


def masked_sums(d, value_of, level, mean, share):
    for t in tiles(d):
        share[t] = inverse_count(d, level, t)
        mean[t] = spread(d, total(masked(live_of(d, level, t), value_of(t)))) * share[t]


def masked_spreads(d, value_of, level, mean, share, scale):
    for t in tiles(d):
        centered = masked(live_of(d, level, t), value_of(t) - across(d, mean, t))
        scale[t] = lax.rsqrt(spread(d, total(centered * centered)) * share[t] + NORM_EPS)


def masked_values(d, value_of, level, mean, scale, gain, bias, low):
    for t in tiles(d):
        unit = (value_of(t) - across(d, mean, t)) * across(d, scale, t)
        low[t] = masked(live_of(d, level, t), unit * gain + bias).astype(BF)


def masked_norm(d, value_of, level, stats, gain, bias, low):
    mean, scale, share = stats[:3]
    masked_sums(d, value_of, level, mean, share)
    masked_spreads(d, value_of, level, mean, share, scale)
    masked_values(d, value_of, level, mean, scale, gain, bias, low)


def masked_back_sums(d, value_of, grad, level, gain, stats):
    mean, scale, first, second = stats
    for t in tiles(d):
        live, share = live_of(d, level, t), inverse_count(d, level, t)
        second[t] = share
        mean[t] = spread(d, total(masked(live, value_of(t)))) * share
        first[t] = spread(d, total(masked(live, grad[t] * gain))) * share
    for t in tiles(d):
        centered = masked(live_of(d, level, t), value_of(t) - across(d, mean, t))
        share = second[t]
        rate = lax.rsqrt(spread(d, total(centered * centered)) * share + NORM_EPS)
        scale[t] = rate
        second[t] = spread(d, total(grad[t] * gain * centered)) * share * rate * rate


def masked_back_value(d, t, value, grad, level, gain, stats):
    mean, scale, first, second = (across(d, ref, t) for ref in stats)
    live = live_of(d, level, t)
    centered = value - mean
    back = masked(live, scale * (grad * gain - first - centered * second))
    live_grad = masked(live, grad)
    return back, live_grad * (centered * scale), live_grad


def plain_sums(d, value_of, mean):
    for t in tiles(d):
        mean[t] = spread(d, total(value_of(t))) * (1.0 / d.ch)


def plain_spreads(d, value_of, mean, scale):
    for t in tiles(d):
        centered = value_of(t) - across(d, mean, t)
        scale[t] = lax.rsqrt(spread(d, total(centered * centered)) * (1.0 / d.ch) + NORM_EPS)


def plain_values(d, value_of, mean, scale, gain, bias, low):
    for t in tiles(d):
        unit = (value_of(t) - across(d, mean, t)) * across(d, scale, t)
        low[t] = (unit * gain + bias).astype(BF)


def plain_back_sums(d, value_of, grad, gain, stats):
    mean, scale, first, second = stats
    for t in tiles(d):
        scaled = grad[t] * gain
        centered = value_of(t) - across(d, mean, t)
        rate = scale[t]
        first[t] = spread(d, total(scaled)) * (1.0 / d.ch)
        second[t] = spread(d, total(scaled * centered)) * (rate * rate * (1.0 / d.ch))


def plain_back_value(d, t, value, grad, gain, stats):
    mean, scale, first, second = (across(d, ref, t) for ref in stats)
    centered = value - mean
    back = scale * (grad * gain - first - centered * second)
    return back, grad * (centered * scale)


def gelu_parts(hidden):
    square = hidden * hidden
    bend = jnp.tanh(hidden * (GELU_SCALE + GELU_SCALE * GELU_CUBE * square))
    return square, bend


def gelu_value(hidden):
    _, bend = gelu_parts(hidden)
    half = 0.5 * hidden
    return half + half * bend


def gelu_both(hidden):
    square, bend = gelu_parts(hidden)
    half = 0.5 * hidden
    slope = half * (GELU_SCALE + (3.0 * GELU_SCALE * GELU_CUBE) * square)
    return half + half * bend, 0.5 + 0.5 * bend + slope * (1.0 - bend * bend)


class Sums:
    def __init__(self):
        self.held = {}

    def add(self, ref, value):
        value = folded(value)
        known = self.held.get(id(ref))
        self.held[id(ref)] = (ref, value if known is None else known[1] + value)

    def store(self):
        for ref, value in self.held.values():
            ref[...] += value


def clear(*refs):
    for ref in refs:
        ref[...] = jnp.zeros_like(ref)


def high_rows(d):
    found, at = [], 0
    for j in range(d.high):
        count = -(-(d.lat - d.bands * j) // 8) * 8
        found.append((j, count, at))
        at += 2 * count
    return found


def high_total(d):
    return 2 * sum(count for _, count, _ in high_rows(d))


def split_parts(d, value):
    value = value.reshape(value.shape[0] // 16, 2, 8, d.ch)
    return [value[:, part].reshape(-1, d.ch) for part in range(2)]


def join_parts(d, real, imag):
    parts = [value.reshape(value.shape[0] // 8, 1, 8, d.ch) for value in (real, imag)]
    return jnp.concatenate(parts, axis=1).reshape(-1, d.ch)


def degrees_to_rows(d, table, arrived_high, arrived):
    @pl.loop(0, d.bands)
    def _(band):
        for j, count, at in high_rows(d):
            real, imag = split_parts(d, arrived_high[band, at : at + 2 * count].astype(F32))
            value = jnp.concatenate([real, imag], axis=1)
            if count < d.lat:
                value = jnp.concatenate([jnp.zeros((d.lat - count, 2 * d.ch), F32), value], axis=0)
            value = matmul_tn(table[band * d.high + j], value.astype(BF))
            rows = join_parts(d, value[:, : d.ch], value[:, d.ch :]).astype(BF)
            for chunk in range(d.chunks):
                arrived[chunk, band, d.low + j] = rows[chunk * 16 : (chunk + 1) * 16]


def rows_to_degrees(d, table, band, send, send_high):
    for j, count, at in high_rows(d):
        rows = [send[chunk, band, d.low + j].astype(F32) for chunk in range(d.chunks)]
        real, imag = split_parts(d, jnp.concatenate(rows, axis=0))
        value = jnp.concatenate([real.astype(BF), imag.astype(BF)], axis=1)
        value = matmul(table[band * d.high + j], value)[d.lat - count :]
        value = join_parts(d, value[:, : d.ch], value[:, d.ch :])
        send_high[band, at : at + 2 * count] = value.astype(BF)


def high_halves(d):
    half = high_total(d) // 32 * 16
    return pl.ds(0, half), pl.ds(half, high_total(d) - half)


def gather_high(d, table, send, send_high, relay, landed_high, sems):
    me = lax.axis_index("space")
    x, y, across_both = sides()
    first, second = high_halves(d)
    rows_to_degrees(d, table, across_both, send, send_high)
    for copy in high_relays(d, send_high, relay, sems):
        copy.start()

    @pl.loop(0, d.bands)
    def _(band):
        @pl.when(band != across_both)
        def _():
            rows_to_degrees(d, table, band, send, send_high)

    for copy in high_relays(d, send_high, relay, sems):
        copy.wait_recv()
    for slot, (band, part) in enumerate(((y, second), (x, first))):
        size = part.size
        value = send_high[band, part].astype(F32) + relay[slot, :size].astype(F32)
        send_high[band, part] = value.astype(BF)
    for copy in high_sends(send_high, landed_high, sems, False):
        copy.start()
    pltpu.make_async_copy(send_high.at[me], landed_high.at[me], sems[2].at[0]).start()


def high_relays(d, send_high, relay, sems):
    x, y, across_both = sides()
    first, second = high_halves(d)
    return [
        side_copy(
            send_high.at[across_both, second], relay.at[0, pl.ds(0, second.size)], sems, 2, x
        ),
        side_copy(
            send_high.at[across_both, first], relay.at[1, pl.ds(0, first.size)], sems, 3, y
        ),
    ]


def high_sends(send_high, landed_high, sems, coming):
    me = lax.axis_index("space")
    x, y, _ = sides()
    return [
        side_copy(send_high.at[peer], landed_high.at[peer if coming else me], sems, slot, peer)
        for slot, peer in enumerate((x, y))
    ]


def finish_high(d, send_high, relay, landed_high, sems):
    me = lax.axis_index("space")
    for copy in high_relays(d, send_high, relay, sems) + high_sends(
        send_high, landed_high, sems, False
    ):
        copy.wait_send()
    for copy in high_sends(send_high, landed_high, sems, True):
        copy.wait_recv()
    pltpu.make_async_copy(send_high.at[me], landed_high.at[me], sems[2].at[0]).wait()


def spread_copies(d, order_high, arrived_high, sems, coming):
    me = lax.axis_index("space")
    x, y, _ = sides()
    return [
        side_copy(order_high, arrived_high.at[peer if coming else me], sems, slot, peer)
        for slot, peer in enumerate((x, y))
    ]


def passing_copies(d, arrived_high, sems, coming):
    x, y, across_both = sides()
    first, second = high_halves(d)
    copies = []
    for slot, peer, origin, part in ((2, x, y, second), (3, y, x, first)):
        target = arrived_high.at[across_both if coming else origin, part]
        copies.append(side_copy(arrived_high.at[origin, part], target, sems, slot, peer))
    return copies


def spread_own(order_high, arrived_high, sems):
    me = lax.axis_index("space")
    return pltpu.make_async_copy(order_high, arrived_high.at[me], sems[2].at[0])


def grid_pieces(d, send, landed, sems):
    def pieces(piece):
        return (
            d.bands,
            piece,
            lambda peer: send.at[piece, peer, pl.ds(0, d.low)],
            lambda band: landed.at[band, :, pl.ds(piece * 2 * d.rows, 2 * d.rows), :],
            sems,
        )

    return pieces


def send_chunk(
    d, at, table, wide, send, send_high, relay, landed, landed_high, sems, high_sems
):
    pieces = grid_pieces(d, send, landed, sems)

    @pl.when(at.step == d.steps - 1)
    def _():
        pack_rows(d, at.chunk, wide, send)
        start_piece(*pieces(at.chunk))

    @pl.when(at.last)
    def _():
        gather_high(d, table, send, send_high, relay, landed_high, high_sems)


def finish_chunks(d, at, send, send_high, relay, landed, landed_high, sems, high_sems):
    @pl.when(at.last)
    def _():
        for piece in range(d.chunks):
            finish_piece(*grid_pieces(d, send, landed, sems)(piece))
        finish_high(d, send_high, relay, landed_high, high_sems)


def order_steps(d):
    return 1 + d.low // d.group


def order_pieces(d, send, arrived, sems):
    count = order_steps(d)

    def first(step):
        part = pl.ds((step - 1) * d.group, d.group)
        return (
            d.bands,
            step - 1,
            lambda peer: send.at[0, peer, part],
            lambda band: arrived.at[0, band, part],
            sems,
        )

    def whole(chunk):
        part = pl.ds(0, d.low)
        return (
            d.bands,
            count + chunk - 2,
            lambda peer: send.at[chunk, peer, part],
            lambda band: arrived.at[chunk, band, part],
            sems,
        )

    return first, whole


PASS_STEP = 5


def send_orders(d, step, peer_count, send, order_high, arrived, arrived_high, sems, high_sems):
    first, whole = order_pieces(d, send, arrived, sems)

    @pl.when(step == 0)
    def _():
        await_peers(peer_count)
        for copy in spread_copies(d, order_high, arrived_high, high_sems, False):
            copy.start()
        spread_own(order_high, arrived_high, high_sems).start()

    @pl.when(step > 0)
    def _():
        start_piece(*first(step))

    @pl.when(step == PASS_STEP)
    def _():
        for copy in spread_copies(d, order_high, arrived_high, high_sems, True):
            copy.wait_recv()
        for copy in passing_copies(d, arrived_high, high_sems, False):
            copy.start()

    @pl.when(step == order_steps(d) - 1)
    def _():
        for chunk in range(1, d.chunks):
            start_piece(*whole(chunk))


def take_chunk(d, at, table, send, order_high, arrived, arrived_high, sems, high_sems, wide):
    first, whole = order_pieces(d, send, arrived, sems)

    @pl.when(at.step == 0)
    def _():
        @pl.when(at.chunk == 0)
        def _():
            for copy in passing_copies(d, arrived_high, high_sems, True):
                copy.wait_recv()
            spread_own(order_high, arrived_high, high_sems).wait()
            degrees_to_rows(d, table, arrived_high, arrived)
            for step in range(1, order_steps(d)):
                finish_piece(*first(step))
            for copy in spread_copies(
                d, order_high, arrived_high, high_sems, False
            ) + passing_copies(d, arrived_high, high_sems, False):
                copy.wait_send()

        @pl.when(at.chunk > 0)
        def _():
            finish_piece(*whole(at.chunk))

        unpack_rows(d, arrived.at[at.chunk], wide)


def pair_copy(source, target, send_sem, recv_sem):
    return pltpu.make_async_remote_copy(
        src_ref=source,
        dst_ref=target,
        send_sem=send_sem,
        recv_sem=recv_sem,
        device_id={"pipe": 1 - lax.axis_index("pipe")},
        device_id_type=MESH,
    )


WEIGHTS = 7
TURN_CHUNK = 3


def point_start_kernel(
    d, edges, mask, gains, biases, orders, *refs
):
    weights = refs[:WEIGHTS]
    x, level, *tables, forward, forward_t, inverse, inverse_t, arrived = refs[WEIGHTS : WEIGHTS + 11]
    fulls = refs[WEIGHTS + 11 : 2 * WEIGHTS + 11]
    (
        landed, landed_high, taken, taken_sems, other_gains, other_biases, swap_out, swap_in, own_sems,
        edge_out, edge_in, turn, mean, scale, share, legendre_rows, low, wide, send, send_high, relay, *sems,
    ) = refs[2 * WEIGHTS + 11 :]
    grid_refs = (send, send_high, relay, landed, landed_high, sems[:3], sems[3:])
    core = lax.axis_index("pipe")
    points = d.sub * d.lon
    piece_points = d.rows * d.lon
    number = pl.program_id(0)
    at = at_of(d, number)
    count = d.chunks * d.steps

    def edge_copy(piece):
        part = pl.ds(piece * piece_points, piece_points)
        return pair_copy(
            edges.at[0, 1 - core, part], arrived.at[part], edge_out.at[piece], edge_in.at[piece]
        )

    def weight_copies(place):
        copies = [
            pair_copy(weights[n].at[0], fulls[n].at[place], swap_out.at[n], swap_in.at[n])
            for n in range(WEIGHTS)
        ]
        copies.append(
            pair_copy(gains, other_gains, swap_out.at[WEIGHTS], swap_in.at[WEIGHTS])
        )
        copies.append(
            pair_copy(biases, other_biases, swap_out.at[WEIGHTS + 1], swap_in.at[WEIGHTS + 1])
        )
        return copies

    def weight_locals():
        return [
            pltpu.make_async_copy(weights[n].at[0], fulls[n].at[core], own_sems.at[n])
            for n in range(WEIGHTS)
        ]

    def take(n, source):
        part = pl.ds(n * points, points)
        slot = lax.rem(n, 2)
        return pltpu.make_async_copy(source.at[part], taken.at[slot], taken_sems.at[slot])

    def start_take(n):
        @pl.when(core == 0)
        def _():
            take(n, edges.at[0, 0]).start()

        @pl.when(core == 1)
        def _():
            @pl.when(lax.rem(n, d.steps) == 0)
            def _():
                edge_copy(n // d.steps).wait_recv()

            take(n, arrived).start()

    def fill():
        lows = orders[: orders.shape[0] - d.bands * d.high]
        legendre_fill(0, lows, d.degrees, 0, *tables[:2], legendre_rows)

    @pl.when(number == 0)
    def _():
        barrier = pltpu.get_barrier_semaphore()
        for peer in peers():
            pl.semaphore_signal(barrier, inc=1, device_id={"space": peer}, device_id_type=MESH)
        pl.semaphore_signal(barrier, inc=1, device_id={"pipe": 1 - core}, device_id_type=MESH)
        pl.semaphore_wait(barrier, d.bands)
        for copy in weight_copies(core) + weight_locals():
            copy.start()
        for piece in range(d.chunks):
            edge_copy(piece).start()
        dft_fill(forward, False, True)
        highs = orders[orders.shape[0] - d.bands * d.high :]
        first_lat = lax.axis_index("space") * d.lat
        legendre_fill(d.degrees - d.lat, highs, d.degrees, first_lat, *tables[2:], legendre_rows)

        @pl.when(core == 1)
        def _():
            fill()
            pl.semaphore_wait(turn, 1)

        start_take(0)
        for copy in weight_copies(1 - core):
            copy.wait_recv()

    @pl.when(number + 1 < count)
    def _():
        start_take(number + 1)

    take(number, edges.at[0, 0]).wait()
    slot = lax.rem(number, 2)
    gain = jnp.where(core == 0, gains[0, 0:1], other_gains[0, 0:1])
    bias = jnp.where(core == 0, biases[0, 0:1], other_biases[0, 0:1])
    value_of = lambda t: x[t].astype(F32)
    for t in tiles(d):
        x[t] = taken[slot, t]
        count = spread(d, total(mask[t].astype(F32)))
        level[t] = (8.0 - count * (8.0 / d.ch)).astype(BF)
    masked_norm(d, value_of, level, (mean, scale, share), gain, bias, low)
    grid_to_modes(d, at, forward, low, wide)
    send_chunk(d, at, tables[2], wide, *grid_refs)

    @pl.when((core == 0) & (at.chunk == TURN_CHUNK) & (at.step == d.steps - 1))
    def _():
        pl.semaphore_signal(turn, inc=1, device_id={"pipe": 1}, device_id_type=MESH)

    @pl.when(at.last)
    def _():
        dft_fill(forward_t, False, False)
        dft_fill(inverse, True, False)
        dft_fill(inverse_t, True, True)

        @pl.when(core == 0)
        def _():
            fill()
            for piece in range(d.chunks):
                edge_copy(piece).wait_recv()

        for piece in range(d.chunks):
            edge_copy(piece).wait_send()
        for copy in weight_copies(core):
            copy.wait_send()
        for copy in weight_locals():
            copy.wait()

    finish_chunks(d, at, *grid_refs)


def point_middle(
    d, at, wide_in, wide, x, level, gains, biases, w_in, b_in, w_out, b_out, inverse, forward,
    residual, output, low, acc, hid, act, mean, scale, share
):
    gain, bias = gains[0, 1:2], biases[0, 1:2]
    modes_to_grid(d, at, inverse, wide_in, acc)
    for t in tiles(d):
        value = x[t].astype(F32) + acc[t]
        residual[t] = value
        mean[t] = spread(d, total(value)) * (1.0 / d.ch)
    value_of = lambda t: residual[t]
    plain_spreads(d, value_of, mean, scale)
    plain_values(d, value_of, mean, scale, gain, bias, low)
    hid[...] = matmul(low[...], w_in[0])
    for t in tiles(d):
        act[t] = gelu_value(hid[t] + b_in[0]).astype(BF)
    acc[...] = matmul(act[...], w_out[0])
    for t in tiles(d):
        output[t] = residual[t] + (acc[t] + b_out[0])
    masked_norm(
        d, lambda t: output[t], level, (mean, scale, share), gains[1, 0:1], biases[1, 0:1], low
    )
    grid_to_modes(d, at, forward, low, wide)


def feed_back(d, layer, sums, refs, low, glow, hid, dact, act, dlow, grads):
    w_in, b_in, w_out = refs
    g_w_in, g_b_in, g_w_out = grads
    hid[...] = matmul(low[...], w_in[layer])
    dact[...] = matmul_nt(glow[...], w_out[layer])
    for t in tiles(d):
        active, slope = gelu_both(hid[t] + b_in[layer])
        act[t] = active.astype(BF)
        d_hidden = dact[t] * slope
        sums.add(g_b_in, d_hidden)
        dlow[t] = d_hidden.astype(BF)
    g_w_out[...] += matmul_tn(act[...], glow[...])
    g_w_in[...] += matmul_tn(low[...], dlow[...])


def point_turn(
    d, at, wide_in, wide, x, held, arrived, gains, biases, w_in, b_in, w_out, b_out, inverse, inverse_t,
    output, d_residual, g_w_in, g_b_in, g_w_out, g_b_out, g_gain, g_bias,
    low, glow, acc, back_acc, hid, dact, act, dlow, mean, scale, first, second
):
    lower = lax.axis_index("pipe") == 0
    gain, bias = gains[1, 1:2], biases[1, 1:2]
    stats = (mean, scale, first, second)
    sums = Sums()
    modes_to_grid(d, at, inverse, wide_in, acc)
    for t in tiles(d):
        value = x[t] + acc[t]
        acc[t] = value
        mean[t] = spread(d, total(value)) * (1.0 / d.ch)
        glow[t] = jnp.where(lower, arrived[t], held[0, t])
    value_of = lambda t: acc[t]
    plain_spreads(d, value_of, mean, scale)
    plain_values(d, value_of, mean, scale, gain, bias, low)
    feed_back(
        d, 1, sums, (w_in, b_in, w_out), low, glow, hid, dact, act, dlow,
        (g_w_in, g_b_in, g_w_out),
    )
    back_acc[...] = matmul_nt(dlow[...], w_in[1])
    dact[:, : d.ch] = matmul(act[...], w_out[1])
    plain_back_sums(d, value_of, back_acc, gain, stats)
    for t in tiles(d):
        value = acc[t]
        final = value + (dact[t, : d.ch] + b_out[1])
        output[0, t] = final.astype(BF)
        upper = glow[t].astype(F32)
        sums.add(g_b_out, upper)
        grad = back_acc[t]
        back, unit_grad = plain_back_value(d, t, value, grad, gain, stats)
        sums.add(g_gain, unit_grad)
        sums.add(g_bias, grad)
        back = upper + back
        d_residual[t] = back
        low[t] = back.astype(BF)
    sums.store()
    grid_to_modes(d, at, inverse_t, low, wide)


def point_back(
    d, at, wide_in, wide, x, level, d_above, residual, gains, biases, w_in, b_in, w_out, forward_t, inverse_t,
    d_residual, g_w_in, g_b_in, g_w_out, g_b_out, g_gain, g_bias, g_gain_above, g_bias_above,
    low, glow, acc, hid, dact, act, dlow, mean, scale, first, second
):
    gain, bias = gains[0, 1:2], biases[0, 1:2]
    gain_above = gains[1, 0:1]
    stats = (mean, scale, first, second)
    sums = Sums()
    modes_to_grid(d, at, forward_t, wide_in, acc)
    masked_back_sums(d, lambda t: x[t], acc, level, gain_above, stats)
    for t in tiles(d):
        back, unit_grad, live_grad = masked_back_value(d, t, x[t], acc[t], level, gain_above, stats)
        sums.add(g_gain_above, unit_grad)
        sums.add(g_bias_above, live_grad)
        upper = d_above[t] + back
        sums.add(g_b_out, upper)
        d_residual[t] = upper
        glow[t] = upper.astype(BF)
    value_of = lambda t: residual[t]
    plain_sums(d, value_of, mean)
    plain_spreads(d, value_of, mean, scale)
    plain_values(d, value_of, mean, scale, gain, bias, low)
    feed_back(
        d, 0, sums, (w_in, b_in, w_out), low, glow, hid, dact, act, dlow,
        (g_w_in, g_b_in, g_w_out),
    )
    acc[...] = matmul_nt(dlow[...], w_in[0])
    plain_back_sums(d, value_of, acc, gain, stats)
    for t in tiles(d):
        grad = acc[t]
        back, unit_grad = plain_back_value(d, t, residual[t], grad, gain, stats)
        sums.add(g_gain, unit_grad)
        sums.add(g_bias, grad)
        back = d_residual[t] + back
        d_residual[t] = back
        low[t] = back.astype(BF)
    sums.store()
    grid_to_modes(d, at, inverse_t, low, wide)


GRADS = 16
GATHER_STEP = 2
SPREAD_STEP = 12


def build_parts(d, grads, parts):
    for layer, held in enumerate((grads[:7], grads[7:])):
        w_in, b_in, w_out, b_out, gain, bias, filters, *above = held
        row = lambda ref, at=0: jnp.sum(ref[:, at : at + d.ch], axis=0, keepdims=True)
        blank = jnp.zeros((2, d.ch), F32)
        first = [row(above[0]), row(above[1])] if above else [blank[:1], blank[1:]]
        small = [first[0], row(gain), first[1], row(bias), row(b_out)]
        small += [row(b_in, at) for at in range(0, d.ff, d.ch)]
        small = jnp.concatenate(small + [jnp.zeros((16 - len(small), d.ch), F32)], axis=0).astype(BF)
        for band in range(d.bands):
            index = layer * d.bands + band
            at = 0
            rows = d.ch // d.bands
            for lane in range(0, d.ff, d.ch):
                value = w_in[band * rows : (band + 1) * rows, lane : lane + d.ch]
                parts[index, at : at + rows] = value.astype(BF)
                at += rows
            rows = d.ff // d.bands
            parts[index, at : at + rows] = w_out[band * rows : (band + 1) * rows].astype(BF)
            at += rows
            lane = band * d.ch // d.bands // 128 * 128
            for part in range(2):
                value = filters[part, :, lane : lane + 128]
                parts[index, at : at + d.degrees, part * 128 : part * 128 + 128] = value.astype(BF)
            at += d.degrees
            parts[index, at : at + 16] = small


def part_rows(d):
    return d.ff // d.bands * 2 + d.degrees + 16


GRADS = 15
GATHER_STEP = 4
SPREAD_STEP = 10


def end_kernel(d, plane, groups, *refs):
    spectral_refs, refs = refs[:7], refs[7:]
    x, level, d_above, gains, forward_t, start_table = refs[:6]
    grads, refs = refs[6 : 6 + GRADS], refs[6 + GRADS :]
    (
        held_in, ends, result, rest, returned,
        acc, mean, scale, first, second, g_filter, wide_in, send, order_high, arrived, arrived_high,
        reply, reply_out, reply_in,
        parts, pair_landed, pair_sum, landed, sum_low, spread_low,
        rest_own, rest_landed, rest_sum, rest_spread,
        out_p, in_p, out_a, in_a, out_b, in_b, out_c, in_c, out_d, in_d, *sems,
    ) = refs
    core, space, dp = lax.axis_index("pipe"), lax.axis_index("space"), lax.axis_index("dp")
    me = core * d.bands + space
    number = pl.program_id(0)
    grads = grads[:6] + (g_filter,) + grads[6:]

    def plane_device(index):
        return {"pipe": index // d.bands, "space": lax.rem(index, d.bands)}

    def copies_to(count, own, device, source, target, outs, ins):
        copies = []
        for shift in range(1, count):
            peer = lax.rem(own + shift, count)
            copies.append(
                pltpu.make_async_remote_copy(
                    src_ref=source(peer),
                    dst_ref=target.at[shift - 1],
                    send_sem=outs.at[shift - 1],
                    recv_sem=ins.at[shift - 1],
                    device_id=device(peer),
                    device_id_type=MESH,
                )
            )
        return copies

    def pair_parts():
        part = pl.ds((1 - core) * d.bands, d.bands)
        return pair_copy(parts.at[part], pair_landed, out_p.at[0], in_p.at[0])

    def band_parts():
        return copies_to(
            d.bands, space, lambda peer: {"space": peer}, lambda peer: pair_sum.at[peer],
            landed, out_a, in_a,
        )

    def shares():
        return copies_to(
            groups, dp, lambda peer: {"dp": peer}, lambda peer: sum_low, spread_low, out_b, in_b
        )

    def rest_copies():
        return copies_to(
            plane, me, plane_device, lambda peer: rest_own, rest_landed, out_c, in_c
        )

    def rest_shares():
        return copies_to(
            groups, dp, lambda peer: {"dp": peer}, lambda peer: rest_sum, rest_spread, out_d, in_d
        )

    def reply_copy(piece, source):
        part = pl.ds(piece * d.rows * d.lon, d.rows * d.lon)
        return pair_copy(source.at[part], returned.at[part], reply_out.at[piece], reply_in.at[piece])

    order_refs = (send, order_high, arrived, arrived_high, sems[:3], sems[3:])
    steps = order_steps(d)

    @pl.when(number == 0)
    def _():
        clear(rest_own, g_filter)
        barrier = pltpu.get_barrier_semaphore()
        for shift in range(1, plane):
            pl.semaphore_signal(
                barrier, inc=1, device_id=plane_device(lax.rem(me + shift, plane)),
                device_id_type=MESH,
            )
        for shift in range(1, groups):
            pl.semaphore_signal(
                barrier, inc=1, device_id={"dp": lax.rem(dp + shift, groups)},
                device_id_type=MESH,
            )
    @pl.when(number < steps)
    def _():
        spectral_back(d, number, send, order_high, *spectral_refs, g_filter)
        send_orders(d, number, plane + groups - 2, *order_refs)

    @pl.when(number >= steps)
    def _():
        at = at_of(d, number - steps)

        @pl.when(at.number == 0)
        def _():
            build_parts(d, grads, parts)
            pair_parts().start()

            @pl.when(core == 0)
            def _():
                for piece in range(d.chunks):
                    reply_copy(piece, held_in.at[1]).start()

        take_chunk(d, at, start_table, *order_refs, wide_in)
        gain = gains[0, 0:1]
        modes_to_grid(d, at, forward_t, wide_in, acc)
        gain_sum, bias_sum = 0.0, 0.0
        points = d.sub * d.lon
        stats = (mean, scale, first, second)
        value_of = lambda t: x[t].astype(F32)
        masked_back_sums(d, value_of, acc, level, gain, stats)
        for t in tiles(d):
            back, unit_grad, live_grad = masked_back_value(
                d, t, value_of(t), acc[t], level, gain, stats
            )
            gain_sum = gain_sum + folded(unit_grad)
            bias_sum = bias_sum + folded(live_grad)
            begin = d_above[t] + back
            begin = begin.astype(BF)
            ends[0, t] = begin
            row = pl.multiple_of(at.number * points + t.start, TILE)
            reply[pl.ds(row, TILE)] = begin
        rest_own[0:8] += gain_sum
        rest_own[8:16] += bias_sum

        @pl.when((core == 1) & (at.step == d.steps - 1))
        def _():
            reply_copy(at.chunk, reply).start()

        @pl.when(at.number == GATHER_STEP)
        def _():
            pair_parts().wait_recv()
            for band in range(d.bands):
                value = parts[core * d.bands + band].astype(F32) + pair_landed[band].astype(F32)
                pair_sum[band] = value.astype(BF)
            for copy in band_parts():
                copy.start()

        @pl.when(at.number == SPREAD_STEP)
        def _():
            for copy in band_parts():
                copy.wait_recv()
            value = pair_sum[space].astype(F32)
            for shift in range(1, d.bands):
                value = value + landed[shift - 1].astype(F32)
            sum_low[...] = value.astype(BF)
            for copy in shares():
                copy.start()

        @pl.when(at.last)
        def _():
            for copy in rest_copies():
                copy.start()
            for copy in shares():
                copy.wait_recv()
            value = sum_low[...].astype(F32)
            for shift in range(1, groups):
                value = value + spread_low[shift - 1].astype(F32)
            result[...] = value
            for copy in rest_copies():
                copy.wait_recv()
            value = rest_own[...]
            for shift in range(1, plane):
                value = value + rest_landed[shift - 1]
            rest_sum[...] = value
            for copy in rest_shares():
                copy.start()
            for copy in rest_shares():
                copy.wait_recv()
            value = rest_sum[...]
            for shift in range(1, groups):
                value = value + rest_spread[shift - 1]
            rest[...] = value
            pair_parts().wait_send()
            for copy in band_parts() + rest_copies() + shares() + rest_shares():
                copy.wait_send()
            for piece in range(d.chunks):

                @pl.when(core == 0)
                def _():
                    reply_copy(piece, held_in.at[1]).wait_send()

                @pl.when(core == 1)
                def _():
                    reply_copy(piece, reply).wait_send()

                reply_copy(piece, held_in.at[1]).wait_recv()


def fused_kernel(d, spectral_part, point_part, counts, cleared, *refs):
    groups, at = [], 0
    for count in counts:
        groups.append(refs[at : at + count])
        at += count
    spectral_in, (start_table, end_table), point_in, spectral_out, point_out, scratch = groups
    (
        landed, landed_high, wide_in, wide, send, send_high, relay, order_high, arrived,
        arrived_high, *sems,
    ) = refs[at:]
    order_refs = (send, order_high, arrived, arrived_high, sems[:3], sems[3:6])
    grid_refs = (send, send_high, relay, landed, landed_high, sems[6:9], sems[9:])
    number = pl.program_id(0)
    steps = order_steps(d)

    @pl.when(number == 0)
    def _():
        greet(d.bands)
        clear(*[(spectral_out + point_out)[n] for n in cleared])

    @pl.when(number < steps)
    def _():
        spectral_part(d, number, send, order_high, *spectral_in, *spectral_out)
        send_orders(d, number, d.bands - 1, *order_refs)

    @pl.when(number >= steps)
    def _():
        at = at_of(d, number - steps)
        take_chunk(d, at, start_table, *order_refs, wide_in)
        point_part(d, at, wide_in, wide, *point_in, *point_out, *scratch)
        send_chunk(d, at, end_table, wide, *grid_refs)
        finish_chunks(d, at, *grid_refs)


def point_index(d, i, lead):
    return jnp.maximum(i - order_steps(d), 0) if lead else i


def sub_spec(d, minor, lead=True):
    return pl.BlockSpec((d.sub * d.lon, minor), lambda i: (point_index(d, i, lead), 0))


def half_spec(d, index):
    return pl.BlockSpec((1, d.sub * d.lon, d.ch), lambda i: (index, point_index(d, i, True), 0))


def whole_spec(shape):
    return pl.BlockSpec(shape, lambda *_: (0,) * len(shape))


ANY_SPEC = pl.BlockSpec(memory_space=pl.ANY)


def sum_shape(d, width):
    return jax.ShapeDtypeStruct((8, width), F32)


def wide_scratch(d):
    return pltpu.VMEM((d.ch // 128, d.rows * lat_stride(d), 128), F32)


def step_scratch(d, minor, kind):
    return pltpu.VMEM((d.sub * d.lon, minor), kind)


def chunk_scratch(d):
    return pltpu.VMEM((d.chunks, d.bands, d.own, 2 * d.rows, d.ch), BF)


def point_cost(d, matmuls, arrays):
    points = d.lat * d.lon
    return pl.CostEstimate(
        flops=int(2 * points * matmuls), bytes_accessed=int(points * d.ch * arrays),
        transcendentals=points * d.ff,
    )


def landed_shapes(d):
    return [
        jax.ShapeDtypeStruct((d.bands, d.low, 2 * d.lat, d.ch), BF),
        jax.ShapeDtypeStruct((d.bands, high_total(d), d.ch), BF),
    ]


def relay_scratch(d):
    return pltpu.VMEM((2, max(part.size for part in high_halves(d)), d.ch), BF)


def high_scratch(d, blocks=None):
    shape = (high_total(d), d.ch)
    return pltpu.VMEM(shape if blocks is None else (blocks,) + shape, BF)


def group_index(d, i):
    return jnp.clip(i - 1, 0, d.low // d.group - 1)


def order_specs(d, layer, sent, tables, coefficients=()):
    analysis, synthesis, filters = tables
    table_spec = pl.BlockSpec(
        (d.group, d.degrees, d.bands * d.lat), lambda i: (group_index(d, i), 0, 0)
    )
    block_spec = pl.BlockSpec(
        (d.bands, d.group, 2 * d.lat, d.ch), lambda i: (0, group_index(d, i), 0, 0)
    )
    specs = [(sent[0], block_spec), (sent[1], None)]
    filter_spec = pl.BlockSpec((1,) + filters.shape[1:], lambda i: (layer, 0, 0, 0))
    specs += [(analysis, table_spec), (synthesis, table_spec), (filters, filter_spec)]
    if coefficients:
        specs += [(coefficients[0], coefficient_spec(d)), (coefficients[1], None)]
    return specs


def coefficient_spec(d):
    return pl.BlockSpec(
        (d.group, d.degrees, 2 * d.ch), lambda i: (group_index(d, i), 0, 0)
    )


def specs_of(pairs):
    return [spec if spec is not None else whole_spec(value.shape) for value, spec in pairs]


def fused_call(
    d, parts, name, collective_id, spectral_in, high_tables, point_in, spectral_out,
    point_out, scratch, cleared, cost,
):
    high_tables = [(table, None) for table in high_tables]
    inputs, outputs = spectral_in + high_tables + point_in, spectral_out + point_out
    counts = [len(v) for v in (spectral_in, high_tables, point_in, spectral_out, point_out)]
    kernel = partial(fused_kernel, d, *parts)

    def body(*refs):
        before = sum(counts)
        landed, after = refs[before : before + 2], refs[before + 2 :]
        held, rest = after[: len(scratch)], after[len(scratch) :]
        kernel(counts + [len(scratch)], cleared, *refs[:before], *held, *landed, *rest)

    return pl.pallas_call(
        body,
        grid=(order_steps(d) + d.chunks * d.steps,),
        in_specs=specs_of(inputs),
        out_specs=specs_of(outputs) + [ANY_SPEC] * 2,
        out_shape=[s for s, _ in outputs] + landed_shapes(d),
        scratch_shapes=scratch
        + [wide_scratch(d), wide_scratch(d), chunk_scratch(d)]
        + [high_scratch(d, d.bands), relay_scratch(d)]
        + [high_scratch(d), chunk_scratch(d), high_scratch(d, d.bands)]
        + exchange_sems(d.bands, order_steps(d) + d.chunks - 2)
        + side_sems()
        + exchange_sems(d.bands, d.chunks)
        + side_sems(),
        compiler_params=pltpu.CompilerParams(
            vmem_limit_bytes=VMEM_BYTES,
            collective_id=collective_id,
            has_side_effects=True,
            dimension_semantics=("arbitrary",),
            fuse_transposed_lhs_in_matmul=True,
        ),
        cost_estimate=cost,
        name=name,
    )(*[a for a, _ in inputs])


def order_rows(d, block, m):
    value = block[:, m].astype(F32).reshape(2 * d.bands * d.lat, d.ch)
    return jnp.concatenate([part.astype(BF) for part in split_parts(d, value)], axis=1)


def place_order(d, m, value, send):
    rows = join_parts(d, value[:, : d.ch], value[:, d.ch :]).astype(BF)
    for band in range(d.bands):
        for chunk in range(d.chunks):
            at = (band * d.chunks + chunk) * 16
            send[chunk, band, m] = rows[at : at + 16]


def filtered(re, im, real, imag):
    return re * real - im * imag, re * imag + im * real


def filtered_back(dr, di, real, imag):
    return dr * real + di * imag, di * real - dr * imag


def spectral(
    d, step, send, send_high, block, block_high, analysis, synthesis, filters,
    coefficients, coefficients_high,
):
    bands = (lax.axis_index("space"),) + sides()[:2]

    @pl.when(step == 0)
    def _():
        for _, count, at in high_rows(d):
            rows = slice(at, at + 2 * count)
            value = sum(block_high[band, rows].astype(F32) for band in bands)
            coefficients_high[rows] = value
            real, imag = (filters[0, part, d.degrees - count :] for part in range(2))
            value = filtered(*split_parts(d, value), real, imag)
            send_high[rows] = join_parts(d, *value).astype(BF)

    @pl.when(step > 0)
    def _():
        real, imag = filters[0, 0], filters[0, 1]
        for m in range(d.group):
            value = matmul(analysis[m], order_rows(d, block, m))
            coefficients[m] = value
            value = filtered(value[:, : d.ch], value[:, d.ch :], real, imag)
            value = jnp.concatenate([part.astype(BF) for part in value], axis=1)
            place_order(d, (step - 1) * d.group + m, matmul_tn(synthesis[m], value), send)


def spectral_back(
    d, step, send, send_high, block, block_high, analysis, synthesis, filters,
    coefficients, coefficients_high, g_filter,
):
    bands = (lax.axis_index("space"),) + sides()[:2]

    @pl.when(step == 0)
    def _():
        for _, count, at in high_rows(d):
            rows = slice(at, at + 2 * count)
            lo = d.degrees - count
            value = sum(block_high[band, rows].astype(F32) for band in bands)
            dr, di = split_parts(d, value)
            re, im = split_parts(d, coefficients_high[rows])
            g_filter[0, lo:] += re * dr + im * di
            g_filter[1, lo:] += re * di - im * dr
            real, imag = (filters[0, part, lo:] for part in range(2))
            send_high[rows] = join_parts(d, *filtered_back(dr, di, real, imag)).astype(BF)

    @pl.when(step > 0)
    def _():
        real, imag = filters[0, 0], filters[0, 1]
        for m in range(d.group):
            value = matmul(synthesis[m], order_rows(d, block, m))
            dr, di = value[:, : d.ch], value[:, d.ch :]
            re, im = coefficients[m, :, : d.ch], coefficients[m, :, d.ch :]
            g_filter[0] += re * dr + im * di
            g_filter[1] += re * di - im * dr
            value = filtered_back(dr, di, real, imag)
            value = jnp.concatenate([part.astype(BF) for part in value], axis=1)
            place_order(d, (step - 1) * d.group + m, matmul_tn(analysis[m], value), send)


def point_start_call(d, edges, mask, own_weights, orders):
    points = d.lat * d.lon
    flat = jax.ShapeDtypeStruct((points, d.ch), BF)
    table = jax.ShapeDtypeStruct((d.low, d.degrees, d.degrees), BF)
    high = jax.ShapeDtypeStruct((d.bands * d.high, d.lat, d.lat), BF)
    fulls = [jax.ShapeDtypeStruct((2,) + w.shape[1:], w.dtype) for w in own_weights]
    gains, biases = own_weights[:2]
    dft = jax.ShapeDtypeStruct((2 * d.own * d.bands, d.lon), BF)
    dma = pltpu.SemaphoreType.DMA
    own = orders.shape[0] - d.bands * d.high
    width = -(-d.degrees // 128) * 128
    rows = max(d.degrees * own, d.lat * d.bands * d.high)
    return pl.pallas_call(
        partial(point_start_kernel, d),
        grid=(d.chunks * d.steps,),
        in_specs=[
            ANY_SPEC,
            sub_spec(d, d.ch, False),
            whole_spec(gains.shape),
            whole_spec(biases.shape),
            whole_spec(orders.shape),
        ]
        + [ANY_SPEC] * WEIGHTS,
        out_specs=[sub_spec(d, d.ch, False), sub_spec(d, 128, False)]
        + [whole_spec(table.shape)] * 2
        + [whole_spec(high.shape)] * 2
        + [whole_spec(dft.shape)] * 4
        + [ANY_SPEC] * (WEIGHTS + 3),
        out_shape=[flat, jax.ShapeDtypeStruct((points, 128), BF), table, table, high, high]
        + [dft] * 4
        + [flat]
        + fulls
        + landed_shapes(d),
        scratch_shapes=[
            pltpu.VMEM((2, d.sub * d.lon, d.ch), BF),
            dma((2,)),
            pltpu.VMEM(gains.shape, F32),
            pltpu.VMEM(biases.shape, F32),
            dma((WEIGHTS + 2,)),
            dma((WEIGHTS + 2,)),
            dma((WEIGHTS,)),
            dma((d.chunks,)),
            dma((d.chunks,)),
            pltpu.SemaphoreType.REGULAR,
            step_scratch(d, 128, F32),
            step_scratch(d, 128, F32),
            step_scratch(d, 128, F32),
            pltpu.VMEM((width // 128, rows, 128), F32),
            step_scratch(d, d.ch, BF),
            wide_scratch(d),
            chunk_scratch(d),
            high_scratch(d, d.bands),
            relay_scratch(d),
        ]
        + exchange_sems(d.bands, d.chunks)
        + side_sems(),
        compiler_params=pltpu.CompilerParams(
            vmem_limit_bytes=VMEM_BYTES,
            collective_id=2,
            has_side_effects=True,
            dimension_semantics=("arbitrary",),
        ),
        cost_estimate=point_cost(d, 2 * d.own * d.bands * d.ch, 8),
        name="point_start",
    )(edges, mask, gains, biases, orders, *own_weights)


def end_call(d, pairs, groups, spectral_in, grid_in, whole_in, grads, held):
    plane = pairs * d.bands
    points = d.lat * d.lon
    shape = (part_rows(d), d.ch)
    rest = (16, d.ch)
    dma = lambda count: [pltpu.SemaphoreType.DMA((max(count, 1),))] * 2
    others = max(groups - 1, 1)
    wholes = [(a, None) for a in whole_in + grads]
    inputs = spectral_in + grid_in + wholes + [(held, ANY_SPEC)]
    return pl.pallas_call(
        partial(end_kernel, d, plane, groups),
        grid=(order_steps(d) + d.chunks * d.steps,),
        in_specs=specs_of(inputs),
        out_specs=[half_spec(d, 0), whole_spec(shape), whole_spec(rest), ANY_SPEC],
        out_shape=[
            jax.ShapeDtypeStruct(held.shape, BF),
            jax.ShapeDtypeStruct(shape, F32),
            jax.ShapeDtypeStruct(rest, F32),
            jax.ShapeDtypeStruct((points, d.ch), BF),
        ],
        scratch_shapes=[step_scratch(d, d.ch, F32)]
        + [step_scratch(d, 128, F32)] * 4
        + [
            pltpu.VMEM((2, d.degrees, d.ch), F32),
            wide_scratch(d),
            chunk_scratch(d),
            high_scratch(d),
            chunk_scratch(d),
            high_scratch(d, d.bands),
            pltpu.VMEM((points, d.ch), BF),
        ]
        + dma(d.chunks)
        + [
            pltpu.VMEM((plane,) + shape, BF),
            pltpu.VMEM((d.bands,) + shape, BF),
            pltpu.VMEM((d.bands,) + shape, BF),
            pltpu.VMEM((d.bands - 1,) + shape, BF),
            pltpu.VMEM(shape, BF),
            pltpu.VMEM((others,) + shape, BF),
            pltpu.VMEM(rest, F32),
            pltpu.VMEM((plane - 1,) + rest, F32),
            pltpu.VMEM(rest, F32),
            pltpu.VMEM((others,) + rest, F32),
        ]
        + dma(1)
        + dma(d.bands - 1)
        + dma(groups - 1)
        + dma(plane - 1)
        + dma(groups - 1)
        + exchange_sems(d.bands, order_steps(d) + d.chunks - 2)
        + side_sems(),
        input_output_aliases={len(inputs) - 1: 0},
        compiler_params=pltpu.CompilerParams(
            vmem_limit_bytes=VMEM_BYTES,
            collective_id=1,
            has_side_effects=True,
            dimension_semantics=("arbitrary",),
            fuse_transposed_lhs_in_matmul=True,
        ),
        cost_estimate=point_cost(d, 2 * d.own * d.bands * d.ch, 18),
        name="spectral_end",
    )(*[a for a, _ in inputs])


def chosen(index, pieces):
    value = pieces[0]
    for n in range(1, len(pieces)):
        value = jnp.where(index == n, pieces[n], value)
    return value


def place_kernel(
    d, where, held, returned, result, rest, ends, g_gain, g_bias, g_filter, g_w_in, g_b_in,
    g_w_out, g_b_out
):
    core, space = where[0], where[1]
    ends[0, core] = held[0].astype(F32)
    ends[0, 1 - core] = returned[...].astype(F32)

    @pl.when(pl.program_id(0) == 0)
    def _():
        at, rows = 0, d.ch // d.bands
        for lane in range(0, d.ff, d.ch):
            g_w_in[0, :, lane : lane + d.ch] = result[at : at + rows]
            at += rows
        rows = d.ff // d.bands
        g_w_out[0] = result[at : at + rows]
        at += rows
        width = d.ch // d.bands
        for part in range(2):
            value = result[at : at + d.degrees, part * 128 : part * 128 + 128].T
            pieces = [value[lane : lane + width] for lane in range(0, 128, width)]
            g_filter[0, part] = chosen(lax.rem(space, len(pieces)), pieces)
        at += d.degrees
        small = result[at : at + 8]
        extra = [jnp.sum(rest[part * 8 : part * 8 + 8], axis=0, keepdims=True) for part in range(2)]
        extra = [jnp.where(core == 0, value, 0.0) for value in extra]
        bands = range(d.bands)

        def cut(row):
            return chosen(space, [row[:, n * width : (n + 1) * width] for n in bands])

        for out, first, more in ((g_gain, 0, extra[0]), (g_bias, 2, extra[1])):
            out[0, 0:1] = cut(small[first : first + 1] + more)
            out[0, 1:2] = cut(small[first + 1 : first + 2])
        g_b_out[...] = cut(small[4:5])
        hidden = [small[5 + n : 6 + n] for n in range(d.ff // d.ch)]
        hidden = jnp.concatenate(hidden, axis=1)
        g_b_in[...] = chosen(space, [hidden[:, n * rows : (n + 1) * rows] for n in bands])


def place_call(d, core, space, held, returned, result, rest, rows):
    points, ch = returned.shape
    width = ch // d.bands
    shapes = [
        (1, 2, points, ch),
        (1, 2, width),
        (1, 2, width),
        (1, 2, width, d.degrees),
        (1, width, d.ff),
        (1, d.ff // d.bands),
        (1, d.ff // d.bands, ch),
        (1, width),
    ]
    return pl.pallas_call(
        partial(place_kernel, d),
        grid_spec=pltpu.PrefetchScalarGridSpec(
            num_scalar_prefetch=1,
            grid=(points // rows,),
            in_specs=[
                pl.BlockSpec((1, rows, ch), lambda i, where: (where[0], i, 0)),
                pl.BlockSpec((rows, ch), lambda i, where: (i, 0)),
                whole_spec(result.shape),
                whole_spec(rest.shape),
            ],
            out_specs=[pl.BlockSpec((1, 2, rows, ch), lambda i, where: (0, 0, i, 0))]
            + [whole_spec(shape) for shape in shapes[1:]],
        ),
        out_shape=[jax.ShapeDtypeStruct(shape, F32) for shape in shapes],
        compiler_params=pltpu.CompilerParams(vmem_limit_bytes=VMEM_BYTES),
        name="place",
    )(jnp.stack([core, space]).astype(jnp.int32), held, returned, result, rest)


def swapped(value, axis, bit):
    mask = 2**bit
    pairs = [(source, source ^ mask) for source in range(lax.axis_size(axis))]
    return lax.ppermute(value, axis, pairs)


def for_sending(shard):
    return jax.tree.map(lambda a: a.astype(jnp.bfloat16) if a.dtype == jnp.float32 else a, shard)


def plain_legendre_table(orders, degree_count, colat_count):
    colatitude = (jnp.arange(colat_count, dtype=jnp.float32) + 0.5) * (math.pi / colat_count)
    cosine = jnp.cos(colatitude)
    sine_col = jnp.sin(colatitude)
    order_value = orders.astype(jnp.float32)[:, None]
    log_start = (
        0.5
        * (
            jnp.log((2.0 * order_value + 1.0) / (4.0 * math.pi))
            + lax.lgamma(order_value + 0.5)
            - lax.lgamma(order_value + 1.0)
            - 0.5 * math.log(math.pi)
        )
        + order_value * jnp.log(sine_col)[None, :]
    )
    start_row = jnp.exp(log_start)

    def recurrence(pair_carry, degree):
        older_row, newer_row = pair_carry
        degree_value = degree.astype(jnp.float32)
        ahead_coef = jnp.sqrt(
            jnp.maximum(4.0 * degree_value * degree_value - 1.0, 0.0)
            / jnp.maximum(degree_value * degree_value - order_value * order_value, 1.0)
        )
        degree_below = degree_value - 1.0
        behind = jnp.sqrt(
            jnp.maximum(degree_below * degree_below - order_value * order_value, 0.0)
            / jnp.maximum(4.0 * degree_below * degree_below - 1.0, 1.0)
        )
        general = ahead_coef * (cosine * newer_row - behind * older_row)
        table_value = jnp.where(
            degree_value < order_value,
            0.0,
            jnp.where(degree_value == order_value, start_row, general),
        )
        return ((newer_row, table_value), table_value)

    zero_rows = jnp.zeros((orders.shape[0], colat_count), jnp.float32)
    last_pair, table_rows = lax.scan(
        recurrence, (zero_rows, zero_rows), jnp.arange(degree_count, dtype=jnp.int32)
    )
    return (jnp.transpose(table_rows, (1, 0, 2)), sine_col)


def plain_fourier_tables(order_count, lon_count):
    orders = jnp.arange(order_count, dtype=jnp.int32)
    points = jnp.arange(lon_count, dtype=jnp.int32)
    phase_index = orders[:, None] * points[None, :] % lon_count
    angle_value = phase_index.astype(jnp.float32) * (2.0 * math.pi / lon_count)
    dft_scale = 2.0 * math.pi / lon_count
    forward = jnp.stack(
        [jnp.cos(angle_value) * dft_scale, -jnp.sin(angle_value) * dft_scale], axis=1
    ).reshape(2 * order_count, lon_count)
    double = jnp.where(orders == 0, 1.0, 2.0).astype(jnp.float32)[:, None]
    inverse = jnp.stack(
        [jnp.cos(angle_value) * double, -jnp.sin(angle_value) * double], axis=1
    ).reshape(2 * order_count, lon_count)
    return (forward, jnp.transpose(inverse))


def norm_masked(values, live_mask, norm_gain, norm_bias):
    live_count = jnp.maximum(jnp.sum(live_mask, axis=-1, keepdims=True), 1.0)
    average = jnp.sum(live_mask * values, axis=-1, keepdims=True) / live_count
    centered = live_mask * (values - average)
    spread = jnp.sum(centered * centered, axis=-1, keepdims=True) / live_count
    return centered * lax.rsqrt(spread + NORM_EPS) * norm_gain + live_mask * norm_bias


def norm_plain(values, norm_gain, norm_bias):
    average = jnp.mean(values, axis=-1, keepdims=True)
    centered = values - average
    spread = jnp.mean(centered * centered, axis=-1, keepdims=True)
    return centered * lax.rsqrt(spread + NORM_EPS) * norm_gain + norm_bias


def filter_modes(coefficients, filter_real, filter_imag):
    real_part = coefficients[:, :, 0]
    imag_part = coefficients[:, :, 1]
    return jnp.stack(
        [
            real_part * filter_real - imag_part * filter_imag,
            real_part * filter_imag + imag_part * filter_real,
        ],
        axis=2,
    )


def split_pairs(moved_data):
    return moved_data.reshape(moved_data.shape[0], moved_data.shape[1] // 2, 2, moved_data.shape[2])


def join_pairs(modal_data):
    return modal_data.reshape(modal_data.shape[0], modal_data.shape[1] * 2, modal_data.shape[3])


def to_modes(spectrum):
    moved_data = lax.all_to_all(spectrum, "space", split_axis=1, concat_axis=0, tiled=True)
    return split_pairs(moved_data)


def to_bands(modal_data):
    joined = join_pairs(modal_data)
    return lax.all_to_all(joined, "space", split_axis=0, concat_axis=1, tiled=True)


def grad_to_modes(spectrum):
    moved_data = lax.all_to_all(spectrum, "space", split_axis=1, concat_axis=0, tiled=True)
    return split_pairs(moved_data)


def grad_to_bands(modal_data):
    joined = join_pairs(modal_data)
    return lax.all_to_all(joined, "space", split_axis=0, concat_axis=1, tiled=True)


def plain_local(edges, mask_levels, norm_gains, norm_biases, filters, w_in, bias_in, w_out, bias_out):
    section_index = lax.axis_index("pipe")
    band_count = lax.axis_size("space")
    micro_count = edges.shape[1]
    lon_count = edges.shape[3]
    channel_count = edges.shape[4]
    lat_count = edges.shape[2] * band_count
    order_count = lon_count // 2
    live_mask = mask_levels.astype(jnp.float32)
    forward_table, inverse_table = plain_fourier_tables(order_count, lon_count)
    forward_dft = forward_table.astype(jnp.bfloat16)
    inverse_dft = inverse_table.astype(jnp.bfloat16)
    order_dev = order_count // band_count
    orders = lax.axis_index("space") * order_dev + jnp.arange(order_dev, dtype=jnp.int32)
    legendre, sine_col = plain_legendre_table(orders, lat_count, lat_count)
    analysis = (legendre * (sine_col * (math.pi / lat_count))[None, None, :]).astype(jnp.bfloat16)
    synthesis = legendre.astype(jnp.bfloat16)
    gelu_tanh = partial(jax.nn.gelu, approximate=True)

    def filter_parts(filter_pair):
        return (filter_pair[0], filter_pair[1])

    def first_norm(values, norm_gain, norm_bias):
        return norm_masked(values, live_mask, norm_gain, norm_bias)

    def forward_layer(values, params):
        gain_pair, bias_pair, filter_pair, weight_in, shift_in, weight_out, shift_out = params
        filter_real, filter_imag = filter_parts(filter_pair)
        normed = first_norm(values, gain_pair[0], bias_pair[0]).astype(jnp.bfloat16)
        spectrum = jnp.einsum(
            "kw,hwc->hkc", forward_dft, normed, preferred_element_type=jnp.float32
        ).astype(jnp.bfloat16)
        modal_data = to_modes(spectrum)
        coefficients = jnp.einsum(
            "mlh,hmrc->mlrc", analysis, modal_data, preferred_element_type=jnp.float32
        )
        filtered = filter_modes(coefficients, filter_real, filter_imag).astype(jnp.bfloat16)
        synthesized = jnp.einsum(
            "mlh,mlrc->hmrc", synthesis, filtered, preferred_element_type=jnp.float32
        ).astype(jnp.bfloat16)
        banded = to_bands(synthesized)
        mixed_grid = jnp.einsum(
            "wk,hkc->hwc", inverse_dft, banded, preferred_element_type=jnp.float32
        )
        residual = values + mixed_grid
        normed_two = (
            norm_plain(residual, gain_pair[1], bias_pair[1])
            .astype(jnp.bfloat16)
            .reshape(-1, channel_count)
        )
        hidden = jnp.dot(normed_two, weight_in, preferred_element_type=jnp.float32) + shift_in
        active = gelu_tanh(hidden).astype(jnp.bfloat16)
        output = jnp.dot(active, weight_out, preferred_element_type=jnp.float32) + shift_out
        saved_state = (values, coefficients, residual, hidden)
        return (residual + output.reshape(values.shape), saved_state)

    def backward_layer(grad_out, saved_state, params):
        gain_pair, bias_pair, filter_pair, weight_in, shift_in, weight_out, shift_out = params
        filter_real, filter_imag = filter_parts(filter_pair)
        values, coefficients, residual, hidden = saved_state
        normed_two_full, norm_two_pull = jax.vjp(norm_plain, residual, gain_pair[1], bias_pair[1])
        normed_two = normed_two_full.astype(jnp.bfloat16).reshape(-1, channel_count)
        active_full, gelu_pull = jax.vjp(gelu_tanh, hidden)
        active = active_full.astype(jnp.bfloat16)
        flat_grad = grad_out.reshape(-1, channel_count)
        grad_shift_out = jnp.sum(flat_grad, axis=0)
        grad_low = flat_grad.astype(jnp.bfloat16)
        grad_weight_out = jnp.einsum(
            "pf,pc->fc", active, grad_low, preferred_element_type=jnp.float32
        )
        grad_active = jnp.einsum(
            "pc,fc->pf", grad_low, weight_out, preferred_element_type=jnp.float32
        )
        grad_hidden = gelu_pull(grad_active)[0]
        grad_shift_in = jnp.sum(grad_hidden, axis=0)
        hidden_low = grad_hidden.astype(jnp.bfloat16)
        grad_weight_in = jnp.einsum(
            "pc,pf->cf", normed_two, hidden_low, preferred_element_type=jnp.float32
        )
        grad_normed_two = jnp.einsum(
            "pf,cf->pc", hidden_low, weight_in, preferred_element_type=jnp.float32
        )
        grad_norm_res, grad_gain_two, grad_bias_two = norm_two_pull(
            grad_normed_two.reshape(residual.shape)
        )
        grad_residual = grad_out + grad_norm_res
        mixed_low = grad_residual.astype(jnp.bfloat16)
        grad_banded = jnp.einsum(
            "wk,hwc->hkc", inverse_dft, mixed_low, preferred_element_type=jnp.float32
        ).astype(jnp.bfloat16)
        grad_modal = grad_to_modes(grad_banded)
        grad_filtered = jnp.einsum(
            "mlh,hmrc->mlrc", synthesis, grad_modal, preferred_element_type=jnp.float32
        )
        filtered_full, filter_pull = jax.vjp(filter_modes, coefficients, filter_real, filter_imag)
        grad_coefficients, grad_filter_real, grad_filter_imag = filter_pull(grad_filtered)
        grad_spectrum = jnp.einsum(
            "mlh,mlrc->hmrc",
            analysis,
            grad_coefficients.astype(jnp.bfloat16),
            preferred_element_type=jnp.float32,
        ).astype(jnp.bfloat16)
        grad_lat = grad_to_bands(grad_spectrum)
        grad_normed = jnp.einsum(
            "kw,hkc->hwc", forward_dft, grad_lat, preferred_element_type=jnp.float32
        )
        normed_full, norm_one_pull = jax.vjp(first_norm, values, gain_pair[0], bias_pair[0])
        grad_norm_in, grad_gain_one, grad_bias_one = norm_one_pull(grad_normed)
        grad_values = grad_residual + grad_norm_in
        layer_grads = (
            jnp.stack([grad_gain_one, grad_gain_two]),
            jnp.stack([grad_bias_one, grad_bias_two]),
            jnp.stack([grad_filter_real, grad_filter_imag]),
            grad_weight_in,
            grad_shift_in,
            grad_weight_out,
            grad_shift_out,
        )
        return (grad_values, layer_grads)

    gathered = (
        lax.all_gather(norm_gains.astype(jnp.bfloat16), "pipe", axis=0, tiled=True).astype(
            norm_gains.dtype
        ),
        lax.all_gather(norm_biases.astype(jnp.bfloat16), "pipe", axis=0, tiled=True).astype(
            norm_biases.dtype
        ),
        lax.all_gather(filters.astype(jnp.bfloat16), "pipe", axis=0, tiled=True).astype(
            filters.dtype
        ),
        lax.all_gather(
            w_in.astype(jnp.float32).astype(jnp.bfloat16), "pipe", axis=0, tiled=True
        ).astype(jnp.float32),
        lax.all_gather(bias_in.astype(jnp.bfloat16), "pipe", axis=0, tiled=True).astype(
            bias_in.dtype
        ),
        lax.all_gather(
            w_out.astype(jnp.float32).astype(jnp.bfloat16), "pipe", axis=0, tiled=True
        ).astype(jnp.float32),
        lax.all_gather(bias_out.astype(jnp.bfloat16), "pipe", axis=0, tiled=True).astype(
            bias_out.dtype
        ),
    )
    all_gains, all_biases, all_filters, all_win, all_bin, all_wout, all_bout = gathered
    layer_params = [
        (
            all_gains[layer_number],
            all_biases[layer_number],
            all_filters[layer_number],
            all_win[layer_number].astype(jnp.bfloat16),
            all_bin[layer_number],
            all_wout[layer_number].astype(jnp.bfloat16),
            all_bout[layer_number],
        )
        for layer_number in range(2)
    ]
    half_count = micro_count // 2
    sending = jnp.where(section_index == 0, edges[0, half_count:], edges[0, :half_count])
    arrived = swapped(sending, "pipe", 0)
    my_inputs = jnp.where(section_index == 0, edges[0, :half_count], arrived)
    my_cotangents = jnp.where(section_index == 0, arrived, edges[0, half_count:])
    first_out, first_state = forward_layer(my_inputs[0].astype(jnp.float32), layer_params[0])
    second_out, second_state = forward_layer(first_out, layer_params[1])
    output_list = [second_out]
    grad_middle, grads_second = backward_layer(
        my_cotangents[0].astype(jnp.float32), second_state, layer_params[1]
    )
    grad_start, grads_first = backward_layer(grad_middle, first_state, layer_params[0])
    grad_list = [grad_start]
    stacked = tuple(
        (
            jnp.stack([first_entry, second_entry])
            for first_entry, second_entry in zip(grads_first, grads_second)
        )
    )
    mine = (
        lax.psum_scatter(
            stacked[0].astype(jnp.bfloat16), "pipe", scatter_dimension=0, tiled=True
        ).astype(jnp.float32),
        lax.psum_scatter(
            stacked[1].astype(jnp.bfloat16), "pipe", scatter_dimension=0, tiled=True
        ).astype(jnp.float32),
        lax.psum_scatter(
            stacked[2].astype(jnp.bfloat16), "pipe", scatter_dimension=0, tiled=True
        ).astype(jnp.float32),
        lax.psum_scatter(
            stacked[3].astype(jnp.bfloat16), "pipe", scatter_dimension=0, tiled=True
        ).astype(jnp.float32),
        lax.psum_scatter(
            stacked[4].astype(jnp.bfloat16), "pipe", scatter_dimension=0, tiled=True
        ).astype(jnp.float32),
        lax.psum_scatter(
            stacked[5].astype(jnp.bfloat16), "pipe", scatter_dimension=0, tiled=True
        ).astype(jnp.float32),
        lax.psum_scatter(
            stacked[6].astype(jnp.bfloat16), "pipe", scatter_dimension=0, tiled=True
        ).astype(jnp.float32),
    )
    totals = tuple((entry[0] for entry in mine))
    output_half = jnp.stack(output_list)
    grad_half = jnp.stack(grad_list)
    reply = jnp.where(section_index == 0, output_half, grad_half)
    returned = swapped(for_sending(reply), "pipe", 0).astype(reply.dtype)
    ends = jnp.where(
        section_index == 0,
        jnp.concatenate([grad_half, returned], axis=0),
        jnp.concatenate([returned, output_half], axis=0),
    )[None]
    gain_grads, bias_grads, filter_grads, win_grads, bin_grads, wout_grads, bout_grads = totals
    gain_part, bias_part, filter_part, win_part, bin_part, wout_part, bout_part = (
        lax.psum_scatter(
            gain_grads.astype(jnp.bfloat16), "space", scatter_dimension=1, tiled=True
        ).astype(jnp.float32),
        lax.psum_scatter(
            bias_grads.astype(jnp.bfloat16), "space", scatter_dimension=1, tiled=True
        ).astype(jnp.float32),
        lax.psum_scatter(
            filter_grads.astype(jnp.bfloat16), "space", scatter_dimension=2, tiled=True
        ).astype(jnp.float32),
        lax.psum_scatter(
            win_grads.astype(jnp.bfloat16), "space", scatter_dimension=0, tiled=True
        ).astype(jnp.float32),
        lax.psum_scatter(
            bin_grads.astype(jnp.bfloat16), "space", scatter_dimension=0, tiled=True
        ).astype(jnp.float32),
        lax.psum_scatter(
            wout_grads.astype(jnp.bfloat16), "space", scatter_dimension=0, tiled=True
        ).astype(jnp.float32),
        lax.psum_scatter(
            bout_grads.astype(jnp.bfloat16), "space", scatter_dimension=0, tiled=True
        ).astype(jnp.float32),
    )
    summed = (
        lax.psum(gain_part.astype(jnp.bfloat16), "dp").astype(jnp.float32),
        lax.psum(bias_part.astype(jnp.bfloat16), "dp").astype(jnp.float32),
        lax.psum(filter_part.astype(jnp.bfloat16), "dp").astype(jnp.float32),
        lax.psum(win_part.astype(jnp.bfloat16), "dp").astype(jnp.float32),
        lax.psum(bin_part.astype(jnp.bfloat16), "dp").astype(jnp.float32),
        lax.psum(wout_part.astype(jnp.bfloat16), "dp").astype(jnp.float32),
        lax.psum(bout_part.astype(jnp.bfloat16), "dp").astype(jnp.float32),
    )
    return (ends,) + tuple((entry[None] for entry in summed))


def local(edges, mask_levels, norm_gains, norm_biases, filters, w_in, bias_in, w_out, bias_out):
    bands = lax.axis_size("space")
    lat, lon, ch = edges.shape[2:]
    odd = lat % ROWS or lat % bands or lon != 2 * lat * bands or bands != 4
    if odd or edges.shape[1] != 2:
        return plain_local(
            edges, mask_levels, norm_gains, norm_biases, filters, w_in, bias_in, w_out, bias_out
        )
    ff = w_in.shape[2]
    orders = lon // 2
    own = orders // bands
    degrees = lat * bands
    sub = 2
    group = 4
    points = lat * lon
    high_count = lat // bands
    low_count = own - high_count
    d = Dims(
        bands, lat, lon, ch, own, degrees, ff, ROWS, lat // ROWS, sub, ROWS // sub, group,
        low_count, high_count,
    )
    core = lax.axis_index("pipe")
    space = lax.axis_index("space")
    edges = edges.reshape(1, 2, points, ch)
    mask = mask_levels.reshape(points, ch)

    low_orders = space + bands * jnp.arange(-(-low_count // 8) * 8, dtype=jnp.int32)
    step = jnp.arange(bands * high_count, dtype=jnp.int32)
    high_orders = bands * (low_count + step % high_count) + step // high_count
    own_weights = (
        norm_gains, norm_biases, filters, w_in, bias_in[:, None, :], w_out, bias_out[:, None, :],
    )
    orders_in = legendre_orders(jnp.concatenate([low_orders, high_orders]))
    x0, level, *made = point_start_call(d, edges, mask, own_weights, orders_in)
    analysis, synthesis, high_analysis, high_synthesis = made[:4]
    forward, forward_t, inverse, inverse_t, arrived = made[4:9]
    gains, biases, filt, win, bin_, wout, bout, *sent = made[9:]

    grid_f32 = (jax.ShapeDtypeStruct((points, ch), F32), sub_spec(d, ch))
    small = lambda *arrays: [(a, None) for a in arrays]
    grid = lambda *arrays: [(a, sub_spec(d, ch)) for a in arrays]
    levels = [(level, sub_spec(d, 128))]
    table = lambda a, b: jax.ShapeDtypeStruct((a, b), F32)
    sums = lambda *widths: [(sum_shape(d, w), None) for w in widths]
    low = step_scratch(d, ch, BF)
    acc = step_scratch(d, ch, F32)
    hid = step_scratch(d, ff, F32)
    act = step_scratch(d, ff, BF)
    stat = step_scratch(d, 128, F32)
    dft = 2 * orders * ch
    ffn = ch * ff
    tables = (analysis, synthesis, filt)
    weight_grads = [(table(ch, ff), None), (sum_shape(d, ff), None), (table(ff, ch), None)]
    coefficients = [
        (jax.ShapeDtypeStruct((low_count, degrees, 2 * ch), F32), coefficient_spec(d)),
        (jax.ShapeDtypeStruct((high_total(d), ch), F32), None),
    ]
    filter_grad = (jax.ShapeDtypeStruct((2, degrees, ch), F32), None)

    *coef0, res0, x1, sent, sent_high = fused_call(
        d, (spectral, point_middle), "spectral_first_point_middle", 3,
        order_specs(d, 0, sent, tables), (high_synthesis, high_analysis),
        grid(x0) + levels + small(gains, biases, win, bin_, wout, bout, inverse, forward),
        coefficients, [grid_f32, grid_f32],
        [low, acc, hid, act, stat, stat, stat], (), point_cost(d, 2 * dft + 2 * ffn, 18),
    )
    held_shape = jax.ShapeDtypeStruct((2, points, ch), BF)
    (
        *coef1, held, d_res1, g_win1, g_bin1, g_wout1, g_bout1, g_gain21, g_bias21, sent,
        sent_high,
    ) = fused_call(
        d, (spectral, point_turn), "spectral_second_point_turn", 4,
        order_specs(d, 1, (sent, sent_high), tables), (high_synthesis, high_synthesis),
        grid(x1) + [(edges[0], half_spec(d, 1))] + grid(arrived)
        + small(gains, biases, win, bin_, wout, bout, inverse, inverse_t),
        coefficients,
        [(held_shape, half_spec(d, 1)), grid_f32] + weight_grads + sums(ch, ch, ch),
        [low, low, acc, acc, hid, hid, act, act, stat, stat, stat, stat],
        (4, 5, 6, 7, 8, 9), point_cost(d, 2 * dft + 6 * ffn, 20),
    )
    (
        g_filt1, d_res0, g_win0, g_bin0, g_wout0, g_bout0, g_gain20, g_bias20, g_gain11, g_bias11,
        sent, sent_high,
    ) = fused_call(
        d, (spectral_back, point_back), "spectral_back_point_back", 5,
        order_specs(d, 1, (sent, sent_high), tables, coef1), (high_analysis, high_synthesis),
        grid(x1) + levels + grid(d_res1, res0)
        + small(gains, biases, win, bin_, wout, forward_t, inverse_t),
        [filter_grad], [grid_f32] + weight_grads + sums(ch, ch, ch, ch, ch),
        [low, low, acc, hid, hid, act, act, stat, stat, stat, stat],
        (0, 2, 3, 4, 5, 6, 7, 8, 9), point_cost(d, 2 * dft + 5 * ffn, 24),
    )
    grads = (
        g_win0, g_bin0, g_wout0, g_bout0, g_gain20, g_bias20,
        g_win1, g_bin1, g_wout1, g_bout1, g_gain21, g_bias21, g_filt1, g_gain11, g_bias11,
    )
    pairs, groups = lax.axis_size("pipe"), lax.axis_size("dp")
    held, result, rest, returned = end_call(
        d, pairs, groups, order_specs(d, 0, (sent, sent_high), tables, coef0),
        grid(x0) + levels + grid(d_res0), (gains, forward_t, high_analysis), grads, held
    )
    ends, *small_grads = place_call(d, core, space, held, returned, result, rest, 4 * lon)
    small_grads[2] = jnp.swapaxes(small_grads[2], 2, 3)
    return (ends.reshape(1, 2, lat, lon, ch), *small_grads)


def solution(mesh):
    return jax.shard_map(
        local,
        mesh=mesh,
        in_specs=(
            P("pipe", "dp", "space", None, None),
            P("space", None, None),
            P("pipe", None, None),
            P("pipe", None, None),
            P("pipe", None, None, None),
            P("pipe", None, None),
            P("pipe", None),
            P("pipe", None, None),
            P("pipe", None),
        ),
        out_specs=(
            P("pipe", "dp", "space", None, None),
            P("pipe", None, "space"),
            P("pipe", None, "space"),
            P("pipe", None, None, "space"),
            P("pipe", "space", None),
            P("pipe", "space"),
            P("pipe", "space", None),
            P("pipe", "space"),
        ),
        check_vma=False,
    )
```

```python
from collections import namedtuple
from functools import partial
import math

import jax
import jax.numpy as jnp
from jax import lax
from jax.experimental import pallas as pl
from jax.experimental.pallas import tpu as pltpu
from jax.sharding import PartitionSpec as P

NORM_EPS = 1e-05
BF = jnp.bfloat16
F32 = jnp.float32
MESH = pl.DeviceIdType.MESH
VMEM_BYTES = 58 * 2**20
TILE = 32
ROWS = 8
GELU_SCALE = math.sqrt(2.0 / math.pi)
GELU_CUBE = 0.044715

Dims = namedtuple(
    "Dims",
    ("bands", "lat", "lon", "ch", "own", "degrees", "ff", "rows", "chunks", "sub", "steps", "group",
     "low", "high"),
)


def matmul(a, b):
    return jnp.dot(a, b, preferred_element_type=F32)


def matmul_tn(a, b):
    return lax.dot_general(a, b, (((0,), (0,)), ((), ())), preferred_element_type=F32)


def matmul_nt(a, b):
    return lax.dot_general(a, b, (((1,), (1,)), ((), ())), preferred_element_type=F32)


def total(value):
    return jnp.sum(value, axis=-1, keepdims=True)


def folded(value):
    return jnp.sum(value.reshape(value.shape[0] // 8, 8, value.shape[1]), axis=0)


def dft_fill(table, inverse, by_order):
    orders, lon = table.shape[0] // 2, table.shape[0]
    order_axis = 0 if by_order else 1
    part = lax.broadcasted_iota(jnp.int32, table.shape, order_axis)
    imaginary = part >= orders
    order = jnp.where(imaginary, part - orders, part).astype(F32)
    point = lax.broadcasted_iota(jnp.int32, table.shape, 1 - order_axis).astype(F32)
    phase = order * point
    phase = phase - lon * jnp.floor(phase * (1.0 / lon))
    phase = jnp.where(phase >= lon, phase - lon, phase)
    angle = phase * (2.0 * math.pi / lon)
    value = jnp.where(imaginary, -jnp.sin(angle), jnp.cos(angle))
    scale = jnp.where(order == 0.0, 1.0, 2.0) if inverse else 2.0 * math.pi / lon
    table[...] = (value * scale).astype(BF)


def legendre_orders(orders):
    order_value = orders.astype(F32)
    factor = 0.5 * (
        jnp.log((2.0 * order_value + 1.0) / (4.0 * math.pi))
        + lax.lgamma(order_value + 0.5)
        - lax.lgamma(order_value + 1.0)
        - 0.5 * math.log(math.pi)
    )
    return jnp.stack([order_value, factor], axis=1)


def legendre_fill(first, orders, colat_count, first_lat, analysis, synthesis, rows):
    count, degrees, lat = analysis.shape
    own, width = orders.shape[0], -(-lat // 128) * 128
    order_value = jnp.broadcast_to(orders[:, 0:1], (own, width))
    square = order_value * order_value
    lats = jnp.minimum(lax.broadcasted_iota(jnp.int32, (8, width), 1) + first_lat, colat_count - 1)
    colatitude = (lats.astype(F32) + 0.5) * (math.pi / colat_count)
    sine = jnp.sin(colatitude)
    cosine = jnp.cos(colatitude)[0:1]
    weight = (sine * (math.pi / colat_count))[0:1]
    start = jnp.exp(orders[:, 1:2] + order_value * jnp.log(sine)[0:1])

    def recurrence(degree, pair):
        older, newer = pair
        value = (degree + first).astype(F32)
        ahead = jnp.sqrt(
            jnp.maximum(4.0 * value * value - 1.0, 0.0) / jnp.maximum(value * value - square, 1.0)
        )
        below = value - 1.0
        behind = jnp.sqrt(
            jnp.maximum(below * below - square, 0.0)
            / jnp.maximum(4.0 * below * below - 1.0, 1.0)
        )
        general = ahead * (cosine * newer - behind * older)
        row = jnp.where(value < order_value, 0.0, jnp.where(value == order_value, start, general))
        at = pl.multiple_of(degree * own, 8)
        for part in range(width // 128):
            rows[part, pl.ds(at, own), :] = row[:, part * 128 : (part + 1) * 128]
        return newer, row

    zero = start * 0.0
    lax.fori_loop(0, degrees, recurrence, (zero, zero))

    @pl.loop(0, count)
    def _(m):
        table = jnp.concatenate(
            [rows[part, pl.ds(m, degrees, stride=own), :] for part in range(width // 128)], axis=1
        )
        synthesis[m] = table[:, :lat].astype(BF)
        analysis[m] = (table * weight)[:, :lat].astype(BF)


def sides():
    me = lax.axis_index("space")
    return me + 1 - 2 * lax.rem(me, 2), lax.rem(me + 2, 4), 3 - me


def peers():
    core = lax.axis_index("pipe")
    x, y, across_both = sides()
    return [across_both, x + core * (y - x), y + core * (x - y)]


def greet(bands):
    barrier = pltpu.get_barrier_semaphore()
    for peer in peers():
        pl.semaphore_signal(barrier, inc=1, device_id={"space": peer}, device_id_type=MESH)


def await_peers(count):
    pl.semaphore_wait(pltpu.get_barrier_semaphore(), count)


def block_copies(bands, piece, source, place, sems, coming):
    out_sems, in_sems, own_sems = sems
    me = lax.axis_index("space")
    copies = []
    for turn, peer in enumerate(peers()):
        band = peer if coming else me
        copies.append(
            pltpu.make_async_remote_copy(
                src_ref=source(peer),
                dst_ref=place(band),
                send_sem=out_sems.at[piece, turn],
                recv_sem=in_sems.at[piece, turn],
                device_id={"space": peer},
                device_id_type=MESH,
            )
        )
    return copies


def own_copy(piece, source, place, sems):
    me = lax.axis_index("space")
    return pltpu.make_async_copy(source(me), place(me), sems[2].at[piece])


def start_piece(bands, piece, source, place, sems):
    for copy in block_copies(bands, piece, source, place, sems, False):
        copy.start()
    own_copy(piece, source, place, sems).start()


def finish_piece(bands, piece, source, place, sems):
    for copy in block_copies(bands, piece, source, place, sems, False):
        copy.wait_send()
    for copy in block_copies(bands, piece, source, place, sems, True):
        copy.wait_recv()
    own_copy(piece, source, place, sems).wait()


def side_copy(source, target, sems, slot, peer):
    return pltpu.make_async_remote_copy(
        src_ref=source,
        dst_ref=target,
        send_sem=sems[0].at[slot],
        recv_sem=sems[1].at[slot],
        device_id={"space": peer},
        device_id_type=MESH,
    )


def side_sems():
    return [pltpu.SemaphoreType.DMA((4,)), pltpu.SemaphoreType.DMA((4,)), pltpu.SemaphoreType.DMA((1,))]


def exchange_sems(bands, pieces):
    return [
        pltpu.SemaphoreType.DMA((pieces, bands - 1)),
        pltpu.SemaphoreType.DMA((pieces, bands - 1)),
        pltpu.SemaphoreType.DMA((pieces,)),
    ]


At = namedtuple("At", ("number", "chunk", "step", "last"))


def at_of(d, number):
    last = number == d.chunks * d.steps - 1
    return At(number, number // d.steps, lax.rem(number, d.steps), last)


def lat_stride(d):
    return 2 * d.bands * d.own + 8


def pack_rows(d, piece, wide, send):
    orders = d.bands * d.own
    for band in range(d.bands):

        @pl.loop(0, d.own, unroll=4)
        def _(m):
            for half in range(d.ch // 128):
                values = []
                for part in range(2):
                    at = part * orders + d.bands * m + band
                    values.append(wide[half, pl.ds(at, d.rows, stride=lat_stride(d)), :])
                lanes = slice(half * 128, half * 128 + 128)
                send[piece, band, m, :, lanes] = jnp.concatenate(values, axis=0).astype(BF)


def unpack_rows(d, block, wide):
    orders = d.bands * d.own
    for band in range(d.bands):

        @pl.loop(0, d.own, unroll=4)
        def _(m):
            value = block[band, m].astype(F32)
            for half in range(d.ch // 128):
                lanes = slice(half * 128, half * 128 + 128)
                for part in range(2):
                    at = part * orders + d.bands * m + band
                    wide[half, pl.ds(at, d.rows, stride=lat_stride(d)), :] = value[
                        part * d.rows : (part + 1) * d.rows, lanes
                    ]


def wide_rows(d, wide, k):
    orders = d.bands * d.own
    at = pl.multiple_of(k * lat_stride(d), 8)
    return jnp.concatenate(
        [wide[half, pl.ds(at, 2 * orders), :].astype(BF) for half in range(d.ch // 128)], axis=1
    )


def store_wide(d, wide, k, value):
    orders = d.bands * d.own
    at = pl.multiple_of(k * lat_stride(d), 8)
    for half in range(d.ch // 128):
        wide[half, pl.ds(at, 2 * orders), :] = value[:, half * 128 : (half + 1) * 128]


def modes_to_grid(d, at, table, wide, acc):
    for s in range(d.sub):
        k = at.step * d.sub + s
        acc[s * d.lon : (s + 1) * d.lon] = matmul(table[...], wide_rows(d, wide, k))


def grid_to_modes(d, at, table, low, wide):
    for s in range(d.sub):
        k = at.step * d.sub + s
        store_wide(d, wide, k, matmul(table[...], low[s * d.lon : (s + 1) * d.lon]))


def tiles(d):
    return [slice(t, t + TILE) for t in range(0, d.sub * d.lon, TILE)]


def spread(d, column):
    return jnp.broadcast_to(column, (TILE, 128))


def across(d, ref, t):
    return jnp.concatenate([ref[t].astype(F32)] * (d.ch // 128), axis=1)


def live_of(d, level, t):
    lane = lax.broadcasted_iota(jnp.int32, (TILE, d.ch), 1)
    return lax.rem(lane, 8).astype(F32) >= across(d, level, t)


def inverse_count(d, level, t):
    return 1.0 / jnp.maximum((d.ch // 8) * (8.0 - level[t].astype(F32)), 1.0)


def masked(live, value):
    return jnp.where(live, value, 0.0)


def masked_sums(d, value_of, level, mean, share):
    for t in tiles(d):
        share[t] = inverse_count(d, level, t)
        mean[t] = spread(d, total(masked(live_of(d, level, t), value_of(t)))) * share[t]


def masked_spreads(d, value_of, level, mean, share, scale):
    for t in tiles(d):
        centered = masked(live_of(d, level, t), value_of(t) - across(d, mean, t))
        scale[t] = lax.rsqrt(spread(d, total(centered * centered)) * share[t] + NORM_EPS)


def masked_values(d, value_of, level, mean, scale, gain, bias, low):
    for t in tiles(d):
        unit = (value_of(t) - across(d, mean, t)) * across(d, scale, t)
        low[t] = masked(live_of(d, level, t), unit * gain + bias).astype(BF)


def masked_norm(d, value_of, level, stats, gain, bias, low):
    mean, scale, share = stats[:3]
    masked_sums(d, value_of, level, mean, share)
    masked_spreads(d, value_of, level, mean, share, scale)
    masked_values(d, value_of, level, mean, scale, gain, bias, low)


def masked_back_sums(d, value_of, grad, level, gain, stats):
    mean, scale, first, second = stats
    for t in tiles(d):
        live, share = live_of(d, level, t), inverse_count(d, level, t)
        second[t] = share
        mean[t] = spread(d, total(masked(live, value_of(t)))) * share
        first[t] = spread(d, total(masked(live, grad[t] * gain))) * share
    for t in tiles(d):
        centered = masked(live_of(d, level, t), value_of(t) - across(d, mean, t))
        share = second[t]
        rate = lax.rsqrt(spread(d, total(centered * centered)) * share + NORM_EPS)
        scale[t] = rate
        second[t] = spread(d, total(grad[t] * gain * centered)) * share * rate * rate


def masked_back_value(d, t, value, grad, level, gain, stats):
    mean, scale, first, second = (across(d, ref, t) for ref in stats)
    live = live_of(d, level, t)
    centered = value - mean
    back = masked(live, scale * (grad * gain - first - centered * second))
    live_grad = masked(live, grad)
    return back, live_grad * (centered * scale), live_grad


def plain_sums(d, value_of, mean):
    for t in tiles(d):
        mean[t] = spread(d, total(value_of(t))) * (1.0 / d.ch)


def plain_spreads(d, value_of, mean, scale):
    for t in tiles(d):
        centered = value_of(t) - across(d, mean, t)
        scale[t] = lax.rsqrt(spread(d, total(centered * centered)) * (1.0 / d.ch) + NORM_EPS)


def plain_values(d, value_of, mean, scale, gain, bias, low):
    for t in tiles(d):
        unit = (value_of(t) - across(d, mean, t)) * across(d, scale, t)
        low[t] = (unit * gain + bias).astype(BF)


def plain_back_sums(d, value_of, grad, gain, stats):
    mean, scale, first, second = stats
    for t in tiles(d):
        scaled = grad[t] * gain
        centered = value_of(t) - across(d, mean, t)
        rate = scale[t]
        first[t] = spread(d, total(scaled)) * (1.0 / d.ch)
        second[t] = spread(d, total(scaled * centered)) * (rate * rate * (1.0 / d.ch))


def plain_back_value(d, t, value, grad, gain, stats):
    mean, scale, first, second = (across(d, ref, t) for ref in stats)
    centered = value - mean
    back = scale * (grad * gain - first - centered * second)
    return back, grad * (centered * scale)


def gelu_parts(hidden):
    square = hidden * hidden
    bend = jnp.tanh(hidden * (GELU_SCALE + GELU_SCALE * GELU_CUBE * square))
    return square, bend


def gelu_value(hidden):
    _, bend = gelu_parts(hidden)
    half = 0.5 * hidden
    return half + half * bend


def gelu_both(hidden):
    square, bend = gelu_parts(hidden)
    half = 0.5 * hidden
    slope = half * (GELU_SCALE + (3.0 * GELU_SCALE * GELU_CUBE) * square)
    return half + half * bend, 0.5 + 0.5 * bend + slope * (1.0 - bend * bend)


class Sums:
    def __init__(self):
        self.held = {}

    def add(self, ref, value):
        value = folded(value)
        known = self.held.get(id(ref))
        self.held[id(ref)] = (ref, value if known is None else known[1] + value)

    def store(self):
        for ref, value in self.held.values():
            ref[...] += value


def clear(*refs):
    for ref in refs:
        ref[...] = jnp.zeros_like(ref)


def high_rows(d):
    found, at = [], 0
    for j in range(d.high):
        count = -(-(d.lat - d.bands * j) // 8) * 8
        found.append((j, count, at))
        at += 2 * count
    return found


def high_total(d):
    return 2 * sum(count for _, count, _ in high_rows(d))


def split_parts(d, value):
    value = value.reshape(value.shape[0] // 16, 2, 8, d.ch)
    return [value[:, part].reshape(-1, d.ch) for part in range(2)]


def join_parts(d, real, imag):
    parts = [value.reshape(value.shape[0] // 8, 1, 8, d.ch) for value in (real, imag)]
    return jnp.concatenate(parts, axis=1).reshape(-1, d.ch)


def degrees_to_rows(d, table, arrived_high, arrived):
    @pl.loop(0, d.bands)
    def _(band):
        for j, count, at in high_rows(d):
            real, imag = split_parts(d, arrived_high[band, at : at + 2 * count].astype(F32))
            value = jnp.concatenate([real, imag], axis=1)
            if count < d.lat:
                value = jnp.concatenate([jnp.zeros((d.lat - count, 2 * d.ch), F32), value], axis=0)
            value = matmul_tn(table[band * d.high + j], value.astype(BF))
            rows = join_parts(d, value[:, : d.ch], value[:, d.ch :]).astype(BF)
            for chunk in range(d.chunks):
                arrived[chunk, band, d.low + j] = rows[chunk * 16 : (chunk + 1) * 16]


def rows_to_degrees(d, table, band, send, send_high):
    for j, count, at in high_rows(d):
        rows = [send[chunk, band, d.low + j].astype(F32) for chunk in range(d.chunks)]
        real, imag = split_parts(d, jnp.concatenate(rows, axis=0))
        value = jnp.concatenate([real.astype(BF), imag.astype(BF)], axis=1)
        value = matmul(table[band * d.high + j], value)[d.lat - count :]
        value = join_parts(d, value[:, : d.ch], value[:, d.ch :])
        send_high[band, at : at + 2 * count] = value.astype(BF)


def high_halves(d):
    half = high_total(d) // 32 * 16
    return pl.ds(0, half), pl.ds(half, high_total(d) - half)


def gather_high(d, table, send, send_high, relay, landed_high, sems):
    me = lax.axis_index("space")
    x, y, across_both = sides()
    first, second = high_halves(d)
    rows_to_degrees(d, table, across_both, send, send_high)
    for copy in high_relays(d, send_high, relay, sems):
        copy.start()

    @pl.loop(0, d.bands)
    def _(band):
        @pl.when(band != across_both)
        def _():
            rows_to_degrees(d, table, band, send, send_high)

    for copy in high_relays(d, send_high, relay, sems):
        copy.wait_recv()
    for slot, (band, part) in enumerate(((y, second), (x, first))):
        size = part.size
        value = send_high[band, part].astype(F32) + relay[slot, :size].astype(F32)
        send_high[band, part] = value.astype(BF)
    for copy in high_sends(send_high, landed_high, sems, False):
        copy.start()
    pltpu.make_async_copy(send_high.at[me], landed_high.at[me], sems[2].at[0]).start()


def high_relays(d, send_high, relay, sems):
    x, y, across_both = sides()
    first, second = high_halves(d)
    return [
        side_copy(
            send_high.at[across_both, second], relay.at[0, pl.ds(0, second.size)], sems, 2, x
        ),
        side_copy(
            send_high.at[across_both, first], relay.at[1, pl.ds(0, first.size)], sems, 3, y
        ),
    ]


def high_sends(send_high, landed_high, sems, coming):
    me = lax.axis_index("space")
    x, y, _ = sides()
    return [
        side_copy(send_high.at[peer], landed_high.at[peer if coming else me], sems, slot, peer)
        for slot, peer in enumerate((x, y))
    ]


def finish_high(d, send_high, relay, landed_high, sems):
    me = lax.axis_index("space")
    for copy in high_relays(d, send_high, relay, sems) + high_sends(
        send_high, landed_high, sems, False
    ):
        copy.wait_send()
    for copy in high_sends(send_high, landed_high, sems, True):
        copy.wait_recv()
    pltpu.make_async_copy(send_high.at[me], landed_high.at[me], sems[2].at[0]).wait()


def spread_copies(d, order_high, arrived_high, sems, coming):
    me = lax.axis_index("space")
    x, y, _ = sides()
    return [
        side_copy(order_high, arrived_high.at[peer if coming else me], sems, slot, peer)
        for slot, peer in enumerate((x, y))
    ]


def passing_copies(d, arrived_high, sems, coming):
    x, y, across_both = sides()
    first, second = high_halves(d)
    copies = []
    for slot, peer, origin, part in ((2, x, y, second), (3, y, x, first)):
        target = arrived_high.at[across_both if coming else origin, part]
        copies.append(side_copy(arrived_high.at[origin, part], target, sems, slot, peer))
    return copies


def spread_own(order_high, arrived_high, sems):
    me = lax.axis_index("space")
    return pltpu.make_async_copy(order_high, arrived_high.at[me], sems[2].at[0])


def grid_pieces(d, send, landed, sems):
    def pieces(piece):
        return (
            d.bands,
            piece,
            lambda peer: send.at[piece, peer, pl.ds(0, d.low)],
            lambda band: landed.at[band, :, pl.ds(piece * 2 * d.rows, 2 * d.rows), :],
            sems,
        )

    return pieces


def send_chunk(
    d, at, table, wide, send, send_high, relay, landed, landed_high, sems, high_sems
):
    pieces = grid_pieces(d, send, landed, sems)

    @pl.when(at.step == d.steps - 1)
    def _():
        pack_rows(d, at.chunk, wide, send)
        start_piece(*pieces(at.chunk))

    @pl.when(at.last)
    def _():
        gather_high(d, table, send, send_high, relay, landed_high, high_sems)


def finish_chunks(d, at, send, send_high, relay, landed, landed_high, sems, high_sems):
    @pl.when(at.last)
    def _():
        for piece in range(d.chunks):
            finish_piece(*grid_pieces(d, send, landed, sems)(piece))
        finish_high(d, send_high, relay, landed_high, high_sems)


def order_steps(d):
    return 1 + d.low // d.group


def order_piece_count(d):
    return EARLY_CHUNKS * (order_steps(d) - 1) + d.chunks - EARLY_CHUNKS


def order_pieces(d, send, arrived, sems):
    groups = order_steps(d) - 1

    def first(step, chunk):
        part = pl.ds((step - 1) * d.group, d.group)
        return (
            d.bands,
            chunk * groups + step - 1,
            lambda peer: send.at[chunk, peer, part],
            lambda band: arrived.at[chunk, band, part],
            sems,
        )

    def whole(chunk):
        part = pl.ds(0, d.low)
        return (
            d.bands,
            EARLY_CHUNKS * groups + chunk - EARLY_CHUNKS,
            lambda peer: send.at[chunk, peer, part],
            lambda band: arrived.at[chunk, band, part],
            sems,
        )

    return first, whole


PASS_STEP = 5
EARLY_CHUNKS = 2


def send_orders(d, step, peer_count, send, order_high, arrived, arrived_high, sems, high_sems):
    first, whole = order_pieces(d, send, arrived, sems)

    @pl.when(step == 0)
    def _():
        await_peers(peer_count)
        for copy in spread_copies(d, order_high, arrived_high, high_sems, False):
            copy.start()
        spread_own(order_high, arrived_high, high_sems).start()

    @pl.when(step > 0)
    def _():
        for chunk in range(EARLY_CHUNKS):
            start_piece(*first(step, chunk))

    @pl.when(step == PASS_STEP)
    def _():
        for copy in spread_copies(d, order_high, arrived_high, high_sems, True):
            copy.wait_recv()
        for copy in passing_copies(d, arrived_high, high_sems, False):
            copy.start()

    @pl.when(step == order_steps(d) - 1)
    def _():
        for chunk in range(EARLY_CHUNKS, d.chunks):
            start_piece(*whole(chunk))


def take_chunk(d, at, table, send, order_high, arrived, arrived_high, sems, high_sems, wide):
    first, whole = order_pieces(d, send, arrived, sems)

    @pl.when(at.step == 0)
    def _():
        @pl.when(at.chunk == 0)
        def _():
            for copy in passing_copies(d, arrived_high, high_sems, True):
                copy.wait_recv()
            spread_own(order_high, arrived_high, high_sems).wait()
            degrees_to_rows(d, table, arrived_high, arrived)
            for copy in spread_copies(
                d, order_high, arrived_high, high_sems, False
            ) + passing_copies(d, arrived_high, high_sems, False):
                copy.wait_send()

        for chunk in range(EARLY_CHUNKS):

            @pl.when(at.chunk == chunk)
            def _():
                for step in range(1, order_steps(d)):
                    finish_piece(*first(step, chunk))

        @pl.when(at.chunk >= EARLY_CHUNKS)
        def _():
            finish_piece(*whole(at.chunk))

        unpack_rows(d, arrived.at[at.chunk], wide)


def pair_copy(source, target, send_sem, recv_sem):
    return pltpu.make_async_remote_copy(
        src_ref=source,
        dst_ref=target,
        send_sem=send_sem,
        recv_sem=recv_sem,
        device_id={"pipe": 1 - lax.axis_index("pipe")},
        device_id_type=MESH,
    )


WEIGHTS = 7
TURN_CHUNK = 3


def point_start_kernel(
    d, edges, mask, gains, biases, orders, *refs
):
    weights = refs[:WEIGHTS]
    x, level, *tables, forward, forward_t, inverse, inverse_t, arrived = refs[WEIGHTS : WEIGHTS + 11]
    fulls = refs[WEIGHTS + 11 : 2 * WEIGHTS + 11]
    (
        landed, landed_high, taken, taken_sems, other_gains, other_biases, swap_out, swap_in, own_sems,
        edge_out, edge_in, turn, mean, scale, share, legendre_rows, low, wide, send, send_high, relay, *sems,
    ) = refs[2 * WEIGHTS + 11 :]
    grid_refs = (send, send_high, relay, landed, landed_high, sems[:3], sems[3:])
    core = lax.axis_index("pipe")
    points = d.sub * d.lon
    piece_points = d.rows * d.lon
    number = pl.program_id(0)
    at = at_of(d, number)
    count = d.chunks * d.steps

    def edge_copy(piece):
        part = pl.ds(piece * piece_points, piece_points)
        return pair_copy(
            edges.at[0, 1 - core, part], arrived.at[part], edge_out.at[piece], edge_in.at[piece]
        )

    def weight_copies(place):
        copies = [
            pair_copy(weights[n].at[0], fulls[n].at[place], swap_out.at[n], swap_in.at[n])
            for n in range(WEIGHTS)
        ]
        copies.append(
            pair_copy(gains, other_gains, swap_out.at[WEIGHTS], swap_in.at[WEIGHTS])
        )
        copies.append(
            pair_copy(biases, other_biases, swap_out.at[WEIGHTS + 1], swap_in.at[WEIGHTS + 1])
        )
        return copies

    def weight_locals():
        return [
            pltpu.make_async_copy(weights[n].at[0], fulls[n].at[core], own_sems.at[n])
            for n in range(WEIGHTS)
        ]

    def take(n, source):
        part = pl.ds(n * points, points)
        slot = lax.rem(n, 2)
        return pltpu.make_async_copy(source.at[part], taken.at[slot], taken_sems.at[slot])

    def start_take(n):
        @pl.when(core == 0)
        def _():
            take(n, edges.at[0, 0]).start()

        @pl.when(core == 1)
        def _():
            @pl.when(lax.rem(n, d.steps) == 0)
            def _():
                edge_copy(n // d.steps).wait_recv()

            take(n, arrived).start()

    def fill():
        lows = orders[: orders.shape[0] - d.bands * d.high]
        legendre_fill(0, lows, d.degrees, 0, *tables[:2], legendre_rows)

    def fill_high():
        highs = orders[orders.shape[0] - d.bands * d.high :]
        first_lat = lax.axis_index("space") * d.lat
        legendre_fill(d.degrees - d.lat, highs, d.degrees, first_lat, *tables[2:], legendre_rows)

    @pl.when(number == 0)
    def _():
        barrier = pltpu.get_barrier_semaphore()
        for peer in peers():
            pl.semaphore_signal(barrier, inc=1, device_id={"space": peer}, device_id_type=MESH)
        pl.semaphore_signal(barrier, inc=1, device_id={"pipe": 1 - core}, device_id_type=MESH)
        pl.semaphore_wait(barrier, d.bands)
        for copy in weight_copies(core) + weight_locals():
            copy.start()
        for piece in range(d.chunks):
            edge_copy(piece).start()
        dft_fill(forward, False, True)

        @pl.when(core == 1)
        def _():
            fill()
            fill_high()
            pl.semaphore_wait(turn, 1)

        start_take(0)
        for copy in weight_copies(1 - core):
            copy.wait_recv()

    @pl.when(number + 1 < count)
    def _():
        start_take(number + 1)

    take(number, edges.at[0, 0]).wait()
    slot = lax.rem(number, 2)
    gain = jnp.where(core == 0, gains[0, 0:1], other_gains[0, 0:1])
    bias = jnp.where(core == 0, biases[0, 0:1], other_biases[0, 0:1])
    value_of = lambda t: x[t].astype(F32)
    for t in tiles(d):
        x[t] = taken[slot, t]
        count = spread(d, total(mask[t].astype(F32)))
        level[t] = (8.0 - count * (8.0 / d.ch)).astype(BF)
    masked_norm(d, value_of, level, (mean, scale, share), gain, bias, low)
    grid_to_modes(d, at, forward, low, wide)

    @pl.when((core == 0) & at.last)
    def _():
        fill_high()

    send_chunk(d, at, tables[2], wide, *grid_refs)

    @pl.when((core == 0) & (at.chunk == TURN_CHUNK) & (at.step == d.steps - 1))
    def _():
        pl.semaphore_signal(turn, inc=1, device_id={"pipe": 1}, device_id_type=MESH)

    @pl.when(at.last)
    def _():
        dft_fill(forward_t, False, False)
        dft_fill(inverse, True, False)
        dft_fill(inverse_t, True, True)

        @pl.when(core == 0)
        def _():
            fill()
            for piece in range(d.chunks):
                edge_copy(piece).wait_recv()

        for piece in range(d.chunks):
            edge_copy(piece).wait_send()
        for copy in weight_copies(core):
            copy.wait_send()
        for copy in weight_locals():
            copy.wait()

    finish_chunks(d, at, *grid_refs)


def point_middle(
    d, at, wide_in, wide, x, level, gains, biases, w_in, b_in, w_out, b_out, inverse, forward,
    residual, output, low, acc, hid, act, mean, scale, share
):
    gain, bias = gains[0, 1:2], biases[0, 1:2]
    modes_to_grid(d, at, inverse, wide_in, acc)
    for t in tiles(d):
        value = x[t].astype(F32) + acc[t]
        residual[t] = value
        mean[t] = spread(d, total(value)) * (1.0 / d.ch)
    value_of = lambda t: residual[t]
    plain_spreads(d, value_of, mean, scale)
    plain_values(d, value_of, mean, scale, gain, bias, low)
    hid[...] = matmul(low[...], w_in[0])
    for t in tiles(d):
        act[t] = gelu_value(hid[t] + b_in[0]).astype(BF)
    acc[...] = matmul(act[...], w_out[0])
    for t in tiles(d):
        output[t] = residual[t] + (acc[t] + b_out[0])
    masked_norm(
        d, lambda t: output[t], level, (mean, scale, share), gains[1, 0:1], biases[1, 0:1], low
    )
    grid_to_modes(d, at, forward, low, wide)


def feed_back(d, layer, sums, refs, low, glow, hid, dact, act, dlow, grads):
    w_in, b_in, w_out = refs
    g_w_in, g_b_in, g_w_out = grads
    hid[...] = matmul(low[...], w_in[layer])
    dact[...] = matmul_nt(glow[...], w_out[layer])
    for t in tiles(d):
        active, slope = gelu_both(hid[t] + b_in[layer])
        act[t] = active.astype(BF)
        d_hidden = dact[t] * slope
        sums.add(g_b_in, d_hidden)
        dlow[t] = d_hidden.astype(BF)
    g_w_out[...] += matmul_tn(act[...], glow[...])
    g_w_in[...] += matmul_tn(low[...], dlow[...])


def point_turn(
    d, at, wide_in, wide, x, held, arrived, gains, biases, w_in, b_in, w_out, b_out, inverse, inverse_t,
    output, d_residual, g_w_in, g_b_in, g_w_out, g_b_out, g_gain, g_bias,
    low, glow, acc, back_acc, hid, dact, act, dlow, mean, scale, first, second
):
    lower = lax.axis_index("pipe") == 0
    gain, bias = gains[1, 1:2], biases[1, 1:2]
    stats = (mean, scale, first, second)
    sums = Sums()
    modes_to_grid(d, at, inverse, wide_in, acc)
    for t in tiles(d):
        value = x[t] + acc[t]
        acc[t] = value
        mean[t] = spread(d, total(value)) * (1.0 / d.ch)
        glow[t] = jnp.where(lower, arrived[t], held[0, t])
    value_of = lambda t: acc[t]
    plain_spreads(d, value_of, mean, scale)
    plain_values(d, value_of, mean, scale, gain, bias, low)
    feed_back(
        d, 1, sums, (w_in, b_in, w_out), low, glow, hid, dact, act, dlow,
        (g_w_in, g_b_in, g_w_out),
    )
    back_acc[...] = matmul_nt(dlow[...], w_in[1])
    dact[:, : d.ch] = matmul(act[...], w_out[1])
    plain_back_sums(d, value_of, back_acc, gain, stats)
    for t in tiles(d):
        value = acc[t]
        final = value + (dact[t, : d.ch] + b_out[1])
        output[0, t] = final.astype(BF)
        upper = glow[t].astype(F32)
        sums.add(g_b_out, upper)
        grad = back_acc[t]
        back, unit_grad = plain_back_value(d, t, value, grad, gain, stats)
        sums.add(g_gain, unit_grad)
        sums.add(g_bias, grad)
        back = upper + back
        d_residual[t] = back
        low[t] = back.astype(BF)
    sums.store()
    grid_to_modes(d, at, inverse_t, low, wide)


def point_back(
    d, at, wide_in, wide, x, level, d_above, residual, gains, biases, w_in, b_in, w_out, forward_t, inverse_t,
    d_residual, g_w_in, g_b_in, g_w_out, g_b_out, g_gain, g_bias, g_gain_above, g_bias_above,
    low, glow, acc, hid, dact, act, dlow, mean, scale, first, second
):
    gain, bias = gains[0, 1:2], biases[0, 1:2]
    gain_above = gains[1, 0:1]
    stats = (mean, scale, first, second)
    sums = Sums()
    modes_to_grid(d, at, forward_t, wide_in, acc)
    masked_back_sums(d, lambda t: x[t], acc, level, gain_above, stats)
    for t in tiles(d):
        back, unit_grad, live_grad = masked_back_value(d, t, x[t], acc[t], level, gain_above, stats)
        sums.add(g_gain_above, unit_grad)
        sums.add(g_bias_above, live_grad)
        upper = d_above[t] + back
        sums.add(g_b_out, upper)
        d_residual[t] = upper
        glow[t] = upper.astype(BF)
    value_of = lambda t: residual[t]
    plain_sums(d, value_of, mean)
    plain_spreads(d, value_of, mean, scale)
    plain_values(d, value_of, mean, scale, gain, bias, low)
    feed_back(
        d, 0, sums, (w_in, b_in, w_out), low, glow, hid, dact, act, dlow,
        (g_w_in, g_b_in, g_w_out),
    )
    acc[...] = matmul_nt(dlow[...], w_in[0])
    plain_back_sums(d, value_of, acc, gain, stats)
    for t in tiles(d):
        grad = acc[t]
        back, unit_grad = plain_back_value(d, t, residual[t], grad, gain, stats)
        sums.add(g_gain, unit_grad)
        sums.add(g_bias, grad)
        back = d_residual[t] + back
        d_residual[t] = back
        low[t] = back.astype(BF)
    sums.store()
    grid_to_modes(d, at, inverse_t, low, wide)


GRADS = 16
GATHER_STEP = 2
SPREAD_STEP = 12


def build_parts(d, grads, parts):
    for layer, held in enumerate((grads[:7], grads[7:])):
        w_in, b_in, w_out, b_out, gain, bias, filters, *above = held
        row = lambda ref, at=0: jnp.sum(ref[:, at : at + d.ch], axis=0, keepdims=True)
        blank = jnp.zeros((2, d.ch), F32)
        first = [row(above[0]), row(above[1])] if above else [blank[:1], blank[1:]]
        small = [first[0], row(gain), first[1], row(bias), row(b_out)]
        small += [row(b_in, at) for at in range(0, d.ff, d.ch)]
        small = jnp.concatenate(small + [jnp.zeros((16 - len(small), d.ch), F32)], axis=0).astype(BF)
        for band in range(d.bands):
            index = layer * d.bands + band
            at = 0
            rows = d.ch // d.bands
            for lane in range(0, d.ff, d.ch):
                value = w_in[band * rows : (band + 1) * rows, lane : lane + d.ch]
                parts[index, at : at + rows] = value.astype(BF)
                at += rows
            rows = d.ff // d.bands
            parts[index, at : at + rows] = w_out[band * rows : (band + 1) * rows].astype(BF)
            at += rows
            lane = band * d.ch // d.bands // 128 * 128
            for part in range(2):
                value = filters[part, :, lane : lane + 128]
                parts[index, at : at + d.degrees, part * 128 : part * 128 + 128] = value.astype(BF)
            at += d.degrees
            parts[index, at : at + 16] = small


def part_rows(d):
    return d.ff // d.bands * 2 + d.degrees + 16


GRADS = 15
GATHER_STEP = 4
SPREAD_STEP = 10


def end_kernel(d, plane, groups, *refs):
    spectral_refs, refs = refs[:7], refs[7:]
    x, level, d_above, gains, forward_t, start_table = refs[:6]
    grads, refs = refs[6 : 6 + GRADS], refs[6 + GRADS :]
    (
        held_in, ends, result, rest, returned,
        acc, mean, scale, first, second, g_filter, wide_in, send, order_high, arrived, arrived_high,
        reply, reply_out, reply_in,
        parts, pair_landed, pair_sum, landed, sum_low, spread_low,
        rest_own, rest_landed, rest_sum, rest_spread,
        out_p, in_p, out_a, in_a, out_b, in_b, out_c, in_c, out_d, in_d, *sems,
    ) = refs
    core, space, dp = lax.axis_index("pipe"), lax.axis_index("space"), lax.axis_index("dp")
    me = core * d.bands + space
    number = pl.program_id(0)
    grads = grads[:6] + (g_filter,) + grads[6:]

    def plane_device(index):
        return {"pipe": index // d.bands, "space": lax.rem(index, d.bands)}

    def copies_to(count, own, device, source, target, outs, ins):
        copies = []
        for shift in range(1, count):
            peer = lax.rem(own + shift, count)
            copies.append(
                pltpu.make_async_remote_copy(
                    src_ref=source(peer),
                    dst_ref=target.at[shift - 1],
                    send_sem=outs.at[shift - 1],
                    recv_sem=ins.at[shift - 1],
                    device_id=device(peer),
                    device_id_type=MESH,
                )
            )
        return copies

    def pair_parts():
        part = pl.ds((1 - core) * d.bands, d.bands)
        return pair_copy(parts.at[part], pair_landed, out_p.at[0], in_p.at[0])

    def band_parts():
        return copies_to(
            d.bands, space, lambda peer: {"space": peer}, lambda peer: pair_sum.at[peer],
            landed, out_a, in_a,
        )

    def shares():
        return copies_to(
            groups, dp, lambda peer: {"dp": peer}, lambda peer: sum_low, spread_low, out_b, in_b
        )

    def rest_copies():
        return copies_to(
            plane, me, plane_device, lambda peer: rest_own, rest_landed, out_c, in_c
        )

    def rest_shares():
        return copies_to(
            groups, dp, lambda peer: {"dp": peer}, lambda peer: rest_sum, rest_spread, out_d, in_d
        )

    def reply_copy(piece, source):
        part = pl.ds(piece * d.rows * d.lon, d.rows * d.lon)
        return pair_copy(source.at[part], returned.at[part], reply_out.at[piece], reply_in.at[piece])

    order_refs = (send, order_high, arrived, arrived_high, sems[:3], sems[3:])
    steps = order_steps(d)

    @pl.when(number == 0)
    def _():
        clear(rest_own, g_filter)
        barrier = pltpu.get_barrier_semaphore()
        for shift in range(1, plane):
            pl.semaphore_signal(
                barrier, inc=1, device_id=plane_device(lax.rem(me + shift, plane)),
                device_id_type=MESH,
            )
        for shift in range(1, groups):
            pl.semaphore_signal(
                barrier, inc=1, device_id={"dp": lax.rem(dp + shift, groups)},
                device_id_type=MESH,
            )
    @pl.when(number < steps)
    def _():
        spectral_back(d, number, send, order_high, *spectral_refs, g_filter)
        send_orders(d, number, plane + groups - 2, *order_refs)

    @pl.when(number >= steps)
    def _():
        at = at_of(d, number - steps)

        @pl.when(at.number == 0)
        def _():
            build_parts(d, grads, parts)
            pair_parts().start()

            @pl.when(core == 0)
            def _():
                for piece in range(d.chunks):
                    reply_copy(piece, held_in.at[1]).start()

        take_chunk(d, at, start_table, *order_refs, wide_in)
        gain = gains[0, 0:1]
        modes_to_grid(d, at, forward_t, wide_in, acc)
        gain_sum, bias_sum = 0.0, 0.0
        points = d.sub * d.lon
        stats = (mean, scale, first, second)
        value_of = lambda t: x[t].astype(F32)
        masked_back_sums(d, value_of, acc, level, gain, stats)
        for t in tiles(d):
            back, unit_grad, live_grad = masked_back_value(
                d, t, value_of(t), acc[t], level, gain, stats
            )
            gain_sum = gain_sum + folded(unit_grad)
            bias_sum = bias_sum + folded(live_grad)
            begin = d_above[t] + back
            begin = begin.astype(BF)
            ends[0, t] = begin
            row = pl.multiple_of(at.number * points + t.start, TILE)
            reply[pl.ds(row, TILE)] = begin
        rest_own[0:8] += gain_sum
        rest_own[8:16] += bias_sum

        @pl.when((core == 1) & (at.step == d.steps - 1))
        def _():
            reply_copy(at.chunk, reply).start()

        @pl.when(at.number == GATHER_STEP)
        def _():
            pair_parts().wait_recv()
            for band in range(d.bands):
                value = parts[core * d.bands + band].astype(F32) + pair_landed[band].astype(F32)
                pair_sum[band] = value.astype(BF)
            for copy in band_parts():
                copy.start()

        @pl.when(at.number == SPREAD_STEP)
        def _():
            for copy in band_parts():
                copy.wait_recv()
            value = pair_sum[space].astype(F32)
            for shift in range(1, d.bands):
                value = value + landed[shift - 1].astype(F32)
            sum_low[...] = value.astype(BF)
            for copy in shares():
                copy.start()

        @pl.when(at.last)
        def _():
            for copy in rest_copies():
                copy.start()
            for copy in shares():
                copy.wait_recv()
            value = sum_low[...].astype(F32)
            for shift in range(1, groups):
                value = value + spread_low[shift - 1].astype(F32)
            result[...] = value
            for copy in rest_copies():
                copy.wait_recv()
            value = rest_own[...]
            for shift in range(1, plane):
                value = value + rest_landed[shift - 1]
            rest_sum[...] = value
            for copy in rest_shares():
                copy.start()
            for copy in rest_shares():
                copy.wait_recv()
            value = rest_sum[...]
            for shift in range(1, groups):
                value = value + rest_spread[shift - 1]
            rest[...] = value
            pair_parts().wait_send()
            for copy in band_parts() + rest_copies() + shares() + rest_shares():
                copy.wait_send()
            for piece in range(d.chunks):

                @pl.when(core == 0)
                def _():
                    reply_copy(piece, held_in.at[1]).wait_send()

                @pl.when(core == 1)
                def _():
                    reply_copy(piece, reply).wait_send()

                reply_copy(piece, held_in.at[1]).wait_recv()


def fused_kernel(d, spectral_part, point_part, counts, cleared, *refs):
    groups, at = [], 0
    for count in counts:
        groups.append(refs[at : at + count])
        at += count
    spectral_in, (start_table, end_table), point_in, spectral_out, point_out, scratch = groups
    (
        landed, landed_high, wide_in, wide, send, send_high, relay, order_high, arrived,
        arrived_high, *sems,
    ) = refs[at:]
    order_refs = (send, order_high, arrived, arrived_high, sems[:3], sems[3:6])
    grid_refs = (send, send_high, relay, landed, landed_high, sems[6:9], sems[9:])
    number = pl.program_id(0)
    steps = order_steps(d)

    @pl.when(number == 0)
    def _():
        greet(d.bands)
        clear(*[(spectral_out + point_out)[n] for n in cleared])

    @pl.when(number < steps)
    def _():
        spectral_part(d, number, send, order_high, *spectral_in, *spectral_out)
        send_orders(d, number, d.bands - 1, *order_refs)

    @pl.when(number >= steps)
    def _():
        at = at_of(d, number - steps)
        take_chunk(d, at, start_table, *order_refs, wide_in)
        point_part(d, at, wide_in, wide, *point_in, *point_out, *scratch)
        send_chunk(d, at, end_table, wide, *grid_refs)
        finish_chunks(d, at, *grid_refs)


def point_index(d, i, lead):
    return jnp.maximum(i - order_steps(d), 0) if lead else i


def sub_spec(d, minor, lead=True):
    return pl.BlockSpec((d.sub * d.lon, minor), lambda i: (point_index(d, i, lead), 0))


def half_spec(d, index):
    return pl.BlockSpec((1, d.sub * d.lon, d.ch), lambda i: (index, point_index(d, i, True), 0))


def whole_spec(shape):
    return pl.BlockSpec(shape, lambda *_: (0,) * len(shape))


ANY_SPEC = pl.BlockSpec(memory_space=pl.ANY)


def sum_shape(d, width):
    return jax.ShapeDtypeStruct((8, width), F32)


def wide_scratch(d):
    return pltpu.VMEM((d.ch // 128, d.rows * lat_stride(d), 128), F32)


def step_scratch(d, minor, kind):
    return pltpu.VMEM((d.sub * d.lon, minor), kind)


def chunk_scratch(d):
    return pltpu.VMEM((d.chunks, d.bands, d.own, 2 * d.rows, d.ch), BF)


def point_cost(d, matmuls, arrays):
    points = d.lat * d.lon
    return pl.CostEstimate(
        flops=int(2 * points * matmuls), bytes_accessed=int(points * d.ch * arrays),
        transcendentals=points * d.ff,
    )


def landed_shapes(d):
    return [
        jax.ShapeDtypeStruct((d.bands, d.low, 2 * d.lat, d.ch), BF),
        jax.ShapeDtypeStruct((d.bands, high_total(d), d.ch), BF),
    ]


def relay_scratch(d):
    return pltpu.VMEM((2, max(part.size for part in high_halves(d)), d.ch), BF)


def high_scratch(d, blocks=None):
    shape = (high_total(d), d.ch)
    return pltpu.VMEM(shape if blocks is None else (blocks,) + shape, BF)


def group_index(d, i):
    return jnp.clip(i - 1, 0, d.low // d.group - 1)


def order_specs(d, layer, sent, tables, coefficients=()):
    analysis, synthesis, filters = tables
    table_spec = pl.BlockSpec(
        (d.group, d.degrees, d.bands * d.lat), lambda i: (group_index(d, i), 0, 0)
    )
    block_spec = pl.BlockSpec(
        (d.bands, d.group, 2 * d.lat, d.ch), lambda i: (0, group_index(d, i), 0, 0)
    )
    specs = [(sent[0], block_spec), (sent[1], None)]
    filter_spec = pl.BlockSpec((1,) + filters.shape[1:], lambda i: (layer, 0, 0, 0))
    specs += [(analysis, table_spec), (synthesis, table_spec), (filters, filter_spec)]
    if coefficients:
        specs += [(coefficients[0], coefficient_spec(d)), (coefficients[1], None)]
    return specs


def coefficient_spec(d):
    return pl.BlockSpec(
        (d.group, d.degrees, 2 * d.ch), lambda i: (group_index(d, i), 0, 0)
    )


def specs_of(pairs):
    return [spec if spec is not None else whole_spec(value.shape) for value, spec in pairs]


def fused_call(
    d, parts, name, collective_id, spectral_in, high_tables, point_in, spectral_out,
    point_out, scratch, cleared, cost,
):
    high_tables = [(table, None) for table in high_tables]
    inputs, outputs = spectral_in + high_tables + point_in, spectral_out + point_out
    counts = [len(v) for v in (spectral_in, high_tables, point_in, spectral_out, point_out)]
    kernel = partial(fused_kernel, d, *parts)

    def body(*refs):
        before = sum(counts)
        landed, after = refs[before : before + 2], refs[before + 2 :]
        held, rest = after[: len(scratch)], after[len(scratch) :]
        kernel(counts + [len(scratch)], cleared, *refs[:before], *held, *landed, *rest)

    return pl.pallas_call(
        body,
        grid=(order_steps(d) + d.chunks * d.steps,),
        in_specs=specs_of(inputs),
        out_specs=specs_of(outputs) + [ANY_SPEC] * 2,
        out_shape=[s for s, _ in outputs] + landed_shapes(d),
        scratch_shapes=scratch
        + [wide_scratch(d), wide_scratch(d), chunk_scratch(d)]
        + [high_scratch(d, d.bands), relay_scratch(d)]
        + [high_scratch(d), chunk_scratch(d), high_scratch(d, d.bands)]
        + exchange_sems(d.bands, order_piece_count(d))
        + side_sems()
        + exchange_sems(d.bands, d.chunks)
        + side_sems(),
        compiler_params=pltpu.CompilerParams(
            vmem_limit_bytes=VMEM_BYTES,
            collective_id=collective_id,
            has_side_effects=True,
            dimension_semantics=("arbitrary",),
            fuse_transposed_lhs_in_matmul=True,
        ),
        cost_estimate=cost,
        name=name,
    )(*[a for a, _ in inputs])


def order_rows(d, block, m):
    value = block[:, m].astype(F32).reshape(2 * d.bands * d.lat, d.ch)
    return jnp.concatenate([part.astype(BF) for part in split_parts(d, value)], axis=1)


def place_order(d, m, value, send):
    rows = join_parts(d, value[:, : d.ch], value[:, d.ch :]).astype(BF)
    for band in range(d.bands):
        for chunk in range(d.chunks):
            at = (band * d.chunks + chunk) * 16
            send[chunk, band, m] = rows[at : at + 16]


def filtered(re, im, real, imag):
    return re * real - im * imag, re * imag + im * real


def filtered_back(dr, di, real, imag):
    return dr * real + di * imag, di * real - dr * imag


def spectral(
    d, step, send, send_high, block, block_high, analysis, synthesis, filters,
    coefficients, coefficients_high,
):
    bands = (lax.axis_index("space"),) + sides()[:2]

    @pl.when(step == 0)
    def _():
        for _, count, at in high_rows(d):
            rows = slice(at, at + 2 * count)
            value = sum(block_high[band, rows].astype(F32) for band in bands)
            coefficients_high[rows] = value
            real, imag = (filters[0, part, d.degrees - count :] for part in range(2))
            value = filtered(*split_parts(d, value), real, imag)
            send_high[rows] = join_parts(d, *value).astype(BF)

    @pl.when(step > 0)
    def _():
        real, imag = filters[0, 0], filters[0, 1]
        for m in range(d.group):
            value = matmul(analysis[m], order_rows(d, block, m))
            coefficients[m] = value
            value = filtered(value[:, : d.ch], value[:, d.ch :], real, imag)
            value = jnp.concatenate([part.astype(BF) for part in value], axis=1)
            place_order(d, (step - 1) * d.group + m, matmul_tn(synthesis[m], value), send)


def spectral_back(
    d, step, send, send_high, block, block_high, analysis, synthesis, filters,
    coefficients, coefficients_high, g_filter,
):
    bands = (lax.axis_index("space"),) + sides()[:2]

    @pl.when(step == 0)
    def _():
        for _, count, at in high_rows(d):
            rows = slice(at, at + 2 * count)
            lo = d.degrees - count
            value = sum(block_high[band, rows].astype(F32) for band in bands)
            dr, di = split_parts(d, value)
            re, im = split_parts(d, coefficients_high[rows])
            g_filter[0, lo:] += re * dr + im * di
            g_filter[1, lo:] += re * di - im * dr
            real, imag = (filters[0, part, lo:] for part in range(2))
            send_high[rows] = join_parts(d, *filtered_back(dr, di, real, imag)).astype(BF)

    @pl.when(step > 0)
    def _():
        real, imag = filters[0, 0], filters[0, 1]
        for m in range(d.group):
            value = matmul(synthesis[m], order_rows(d, block, m))
            dr, di = value[:, : d.ch], value[:, d.ch :]
            re, im = coefficients[m, :, : d.ch], coefficients[m, :, d.ch :]
            g_filter[0] += re * dr + im * di
            g_filter[1] += re * di - im * dr
            value = filtered_back(dr, di, real, imag)
            value = jnp.concatenate([part.astype(BF) for part in value], axis=1)
            place_order(d, (step - 1) * d.group + m, matmul_tn(analysis[m], value), send)


def point_start_call(d, edges, mask, own_weights, orders):
    points = d.lat * d.lon
    flat = jax.ShapeDtypeStruct((points, d.ch), BF)
    table = jax.ShapeDtypeStruct((d.low, d.degrees, d.degrees), BF)
    high = jax.ShapeDtypeStruct((d.bands * d.high, d.lat, d.lat), BF)
    fulls = [jax.ShapeDtypeStruct((2,) + w.shape[1:], w.dtype) for w in own_weights]
    gains, biases = own_weights[:2]
    dft = jax.ShapeDtypeStruct((2 * d.own * d.bands, d.lon), BF)
    dma = pltpu.SemaphoreType.DMA
    own = orders.shape[0] - d.bands * d.high
    width = -(-d.degrees // 128) * 128
    rows = max(d.degrees * own, d.lat * d.bands * d.high)
    return pl.pallas_call(
        partial(point_start_kernel, d),
        grid=(d.chunks * d.steps,),
        in_specs=[
            ANY_SPEC,
            sub_spec(d, d.ch, False),
            whole_spec(gains.shape),
            whole_spec(biases.shape),
            whole_spec(orders.shape),
        ]
        + [ANY_SPEC] * WEIGHTS,
        out_specs=[sub_spec(d, d.ch, False), sub_spec(d, 128, False)]
        + [whole_spec(table.shape)] * 2
        + [whole_spec(high.shape)] * 2
        + [whole_spec(dft.shape)] * 4
        + [ANY_SPEC] * (WEIGHTS + 3),
        out_shape=[flat, jax.ShapeDtypeStruct((points, 128), BF), table, table, high, high]
        + [dft] * 4
        + [flat]
        + fulls
        + landed_shapes(d),
        scratch_shapes=[
            pltpu.VMEM((2, d.sub * d.lon, d.ch), BF),
            dma((2,)),
            pltpu.VMEM(gains.shape, F32),
            pltpu.VMEM(biases.shape, F32),
            dma((WEIGHTS + 2,)),
            dma((WEIGHTS + 2,)),
            dma((WEIGHTS,)),
            dma((d.chunks,)),
            dma((d.chunks,)),
            pltpu.SemaphoreType.REGULAR,
            step_scratch(d, 128, F32),
            step_scratch(d, 128, F32),
            step_scratch(d, 128, F32),
            pltpu.VMEM((width // 128, rows, 128), F32),
            step_scratch(d, d.ch, BF),
            wide_scratch(d),
            chunk_scratch(d),
            high_scratch(d, d.bands),
            relay_scratch(d),
        ]
        + exchange_sems(d.bands, d.chunks)
        + side_sems(),
        compiler_params=pltpu.CompilerParams(
            vmem_limit_bytes=VMEM_BYTES,
            collective_id=2,
            has_side_effects=True,
            dimension_semantics=("arbitrary",),
        ),
        cost_estimate=point_cost(d, 2 * d.own * d.bands * d.ch, 8),
        name="point_start",
    )(edges, mask, gains, biases, orders, *own_weights)


def end_call(d, pairs, groups, spectral_in, grid_in, whole_in, grads, held):
    plane = pairs * d.bands
    points = d.lat * d.lon
    shape = (part_rows(d), d.ch)
    rest = (16, d.ch)
    dma = lambda count: [pltpu.SemaphoreType.DMA((max(count, 1),))] * 2
    others = max(groups - 1, 1)
    wholes = [(a, None) for a in whole_in + grads]
    inputs = spectral_in + grid_in + wholes + [(held, ANY_SPEC)]
    return pl.pallas_call(
        partial(end_kernel, d, plane, groups),
        grid=(order_steps(d) + d.chunks * d.steps,),
        in_specs=specs_of(inputs),
        out_specs=[half_spec(d, 0), whole_spec(shape), whole_spec(rest), ANY_SPEC],
        out_shape=[
            jax.ShapeDtypeStruct(held.shape, BF),
            jax.ShapeDtypeStruct(shape, F32),
            jax.ShapeDtypeStruct(rest, F32),
            jax.ShapeDtypeStruct((points, d.ch), BF),
        ],
        scratch_shapes=[step_scratch(d, d.ch, F32)]
        + [step_scratch(d, 128, F32)] * 4
        + [
            pltpu.VMEM((2, d.degrees, d.ch), F32),
            wide_scratch(d),
            chunk_scratch(d),
            high_scratch(d),
            chunk_scratch(d),
            high_scratch(d, d.bands),
            pltpu.VMEM((points, d.ch), BF),
        ]
        + dma(d.chunks)
        + [
            pltpu.VMEM((plane,) + shape, BF),
            pltpu.VMEM((d.bands,) + shape, BF),
            pltpu.VMEM((d.bands,) + shape, BF),
            pltpu.VMEM((d.bands - 1,) + shape, BF),
            pltpu.VMEM(shape, BF),
            pltpu.VMEM((others,) + shape, BF),
            pltpu.VMEM(rest, F32),
            pltpu.VMEM((plane - 1,) + rest, F32),
            pltpu.VMEM(rest, F32),
            pltpu.VMEM((others,) + rest, F32),
        ]
        + dma(1)
        + dma(d.bands - 1)
        + dma(groups - 1)
        + dma(plane - 1)
        + dma(groups - 1)
        + exchange_sems(d.bands, order_piece_count(d))
        + side_sems(),
        input_output_aliases={len(inputs) - 1: 0},
        compiler_params=pltpu.CompilerParams(
            vmem_limit_bytes=VMEM_BYTES,
            collective_id=1,
            has_side_effects=True,
            dimension_semantics=("arbitrary",),
            fuse_transposed_lhs_in_matmul=True,
        ),
        cost_estimate=point_cost(d, 2 * d.own * d.bands * d.ch, 18),
        name="spectral_end",
    )(*[a for a, _ in inputs])


def chosen(index, pieces):
    value = pieces[0]
    for n in range(1, len(pieces)):
        value = jnp.where(index == n, pieces[n], value)
    return value


def place_kernel(
    d, where, held, returned, result, rest, ends, g_gain, g_bias, g_filter, g_w_in, g_b_in,
    g_w_out, g_b_out
):
    core, space = where[0], where[1]
    ends[0, core] = held[0].astype(F32)
    ends[0, 1 - core] = returned[...].astype(F32)

    @pl.when(pl.program_id(0) == 0)
    def _():
        at, rows = 0, d.ch // d.bands
        for lane in range(0, d.ff, d.ch):
            g_w_in[0, :, lane : lane + d.ch] = result[at : at + rows]
            at += rows
        rows = d.ff // d.bands
        g_w_out[0] = result[at : at + rows]
        at += rows
        width = d.ch // d.bands
        for part in range(2):
            value = result[at : at + d.degrees, part * 128 : part * 128 + 128].T
            pieces = [value[lane : lane + width] for lane in range(0, 128, width)]
            g_filter[0, part] = chosen(lax.rem(space, len(pieces)), pieces)
        at += d.degrees
        small = result[at : at + 8]
        extra = [jnp.sum(rest[part * 8 : part * 8 + 8], axis=0, keepdims=True) for part in range(2)]
        extra = [jnp.where(core == 0, value, 0.0) for value in extra]
        bands = range(d.bands)

        def cut(row):
            return chosen(space, [row[:, n * width : (n + 1) * width] for n in bands])

        for out, first, more in ((g_gain, 0, extra[0]), (g_bias, 2, extra[1])):
            out[0, 0:1] = cut(small[first : first + 1] + more)
            out[0, 1:2] = cut(small[first + 1 : first + 2])
        g_b_out[...] = cut(small[4:5])
        hidden = [small[5 + n : 6 + n] for n in range(d.ff // d.ch)]
        hidden = jnp.concatenate(hidden, axis=1)
        g_b_in[...] = chosen(space, [hidden[:, n * rows : (n + 1) * rows] for n in bands])


def place_call(d, core, space, held, returned, result, rest, rows):
    points, ch = returned.shape
    width = ch // d.bands
    shapes = [
        (1, 2, points, ch),
        (1, 2, width),
        (1, 2, width),
        (1, 2, width, d.degrees),
        (1, width, d.ff),
        (1, d.ff // d.bands),
        (1, d.ff // d.bands, ch),
        (1, width),
    ]
    return pl.pallas_call(
        partial(place_kernel, d),
        grid_spec=pltpu.PrefetchScalarGridSpec(
            num_scalar_prefetch=1,
            grid=(points // rows,),
            in_specs=[
                pl.BlockSpec((1, rows, ch), lambda i, where: (where[0], i, 0)),
                pl.BlockSpec((rows, ch), lambda i, where: (i, 0)),
                whole_spec(result.shape),
                whole_spec(rest.shape),
            ],
            out_specs=[pl.BlockSpec((1, 2, rows, ch), lambda i, where: (0, 0, i, 0))]
            + [whole_spec(shape) for shape in shapes[1:]],
        ),
        out_shape=[jax.ShapeDtypeStruct(shape, F32) for shape in shapes],
        compiler_params=pltpu.CompilerParams(vmem_limit_bytes=VMEM_BYTES),
        name="place",
    )(jnp.stack([core, space]).astype(jnp.int32), held, returned, result, rest)


def swapped(value, axis, bit):
    mask = 2**bit
    pairs = [(source, source ^ mask) for source in range(lax.axis_size(axis))]
    return lax.ppermute(value, axis, pairs)


def for_sending(shard):
    return jax.tree.map(lambda a: a.astype(jnp.bfloat16) if a.dtype == jnp.float32 else a, shard)


def plain_legendre_table(orders, degree_count, colat_count):
    colatitude = (jnp.arange(colat_count, dtype=jnp.float32) + 0.5) * (math.pi / colat_count)
    cosine = jnp.cos(colatitude)
    sine_col = jnp.sin(colatitude)
    order_value = orders.astype(jnp.float32)[:, None]
    log_start = (
        0.5
        * (
            jnp.log((2.0 * order_value + 1.0) / (4.0 * math.pi))
            + lax.lgamma(order_value + 0.5)
            - lax.lgamma(order_value + 1.0)
            - 0.5 * math.log(math.pi)
        )
        + order_value * jnp.log(sine_col)[None, :]
    )
    start_row = jnp.exp(log_start)

    def recurrence(pair_carry, degree):
        older_row, newer_row = pair_carry
        degree_value = degree.astype(jnp.float32)
        ahead_coef = jnp.sqrt(
            jnp.maximum(4.0 * degree_value * degree_value - 1.0, 0.0)
            / jnp.maximum(degree_value * degree_value - order_value * order_value, 1.0)
        )
        degree_below = degree_value - 1.0
        behind = jnp.sqrt(
            jnp.maximum(degree_below * degree_below - order_value * order_value, 0.0)
            / jnp.maximum(4.0 * degree_below * degree_below - 1.0, 1.0)
        )
        general = ahead_coef * (cosine * newer_row - behind * older_row)
        table_value = jnp.where(
            degree_value < order_value,
            0.0,
            jnp.where(degree_value == order_value, start_row, general),
        )
        return ((newer_row, table_value), table_value)

    zero_rows = jnp.zeros((orders.shape[0], colat_count), jnp.float32)
    last_pair, table_rows = lax.scan(
        recurrence, (zero_rows, zero_rows), jnp.arange(degree_count, dtype=jnp.int32)
    )
    return (jnp.transpose(table_rows, (1, 0, 2)), sine_col)


def plain_fourier_tables(order_count, lon_count):
    orders = jnp.arange(order_count, dtype=jnp.int32)
    points = jnp.arange(lon_count, dtype=jnp.int32)
    phase_index = orders[:, None] * points[None, :] % lon_count
    angle_value = phase_index.astype(jnp.float32) * (2.0 * math.pi / lon_count)
    dft_scale = 2.0 * math.pi / lon_count
    forward = jnp.stack(
        [jnp.cos(angle_value) * dft_scale, -jnp.sin(angle_value) * dft_scale], axis=1
    ).reshape(2 * order_count, lon_count)
    double = jnp.where(orders == 0, 1.0, 2.0).astype(jnp.float32)[:, None]
    inverse = jnp.stack(
        [jnp.cos(angle_value) * double, -jnp.sin(angle_value) * double], axis=1
    ).reshape(2 * order_count, lon_count)
    return (forward, jnp.transpose(inverse))


def norm_masked(values, live_mask, norm_gain, norm_bias):
    live_count = jnp.maximum(jnp.sum(live_mask, axis=-1, keepdims=True), 1.0)
    average = jnp.sum(live_mask * values, axis=-1, keepdims=True) / live_count
    centered = live_mask * (values - average)
    spread = jnp.sum(centered * centered, axis=-1, keepdims=True) / live_count
    return centered * lax.rsqrt(spread + NORM_EPS) * norm_gain + live_mask * norm_bias


def norm_plain(values, norm_gain, norm_bias):
    average = jnp.mean(values, axis=-1, keepdims=True)
    centered = values - average
    spread = jnp.mean(centered * centered, axis=-1, keepdims=True)
    return centered * lax.rsqrt(spread + NORM_EPS) * norm_gain + norm_bias


def filter_modes(coefficients, filter_real, filter_imag):
    real_part = coefficients[:, :, 0]
    imag_part = coefficients[:, :, 1]
    return jnp.stack(
        [
            real_part * filter_real - imag_part * filter_imag,
            real_part * filter_imag + imag_part * filter_real,
        ],
        axis=2,
    )


def split_pairs(moved_data):
    return moved_data.reshape(moved_data.shape[0], moved_data.shape[1] // 2, 2, moved_data.shape[2])


def join_pairs(modal_data):
    return modal_data.reshape(modal_data.shape[0], modal_data.shape[1] * 2, modal_data.shape[3])


def to_modes(spectrum):
    moved_data = lax.all_to_all(spectrum, "space", split_axis=1, concat_axis=0, tiled=True)
    return split_pairs(moved_data)


def to_bands(modal_data):
    joined = join_pairs(modal_data)
    return lax.all_to_all(joined, "space", split_axis=0, concat_axis=1, tiled=True)


def grad_to_modes(spectrum):
    moved_data = lax.all_to_all(spectrum, "space", split_axis=1, concat_axis=0, tiled=True)
    return split_pairs(moved_data)


def grad_to_bands(modal_data):
    joined = join_pairs(modal_data)
    return lax.all_to_all(joined, "space", split_axis=0, concat_axis=1, tiled=True)


def plain_local(edges, mask_levels, norm_gains, norm_biases, filters, w_in, bias_in, w_out, bias_out):
    section_index = lax.axis_index("pipe")
    band_count = lax.axis_size("space")
    micro_count = edges.shape[1]
    lon_count = edges.shape[3]
    channel_count = edges.shape[4]
    lat_count = edges.shape[2] * band_count
    order_count = lon_count // 2
    live_mask = mask_levels.astype(jnp.float32)
    forward_table, inverse_table = plain_fourier_tables(order_count, lon_count)
    forward_dft = forward_table.astype(jnp.bfloat16)
    inverse_dft = inverse_table.astype(jnp.bfloat16)
    order_dev = order_count // band_count
    orders = lax.axis_index("space") * order_dev + jnp.arange(order_dev, dtype=jnp.int32)
    legendre, sine_col = plain_legendre_table(orders, lat_count, lat_count)
    analysis = (legendre * (sine_col * (math.pi / lat_count))[None, None, :]).astype(jnp.bfloat16)
    synthesis = legendre.astype(jnp.bfloat16)
    gelu_tanh = partial(jax.nn.gelu, approximate=True)

    def filter_parts(filter_pair):
        return (filter_pair[0], filter_pair[1])

    def first_norm(values, norm_gain, norm_bias):
        return norm_masked(values, live_mask, norm_gain, norm_bias)

    def forward_layer(values, params):
        gain_pair, bias_pair, filter_pair, weight_in, shift_in, weight_out, shift_out = params
        filter_real, filter_imag = filter_parts(filter_pair)
        normed = first_norm(values, gain_pair[0], bias_pair[0]).astype(jnp.bfloat16)
        spectrum = jnp.einsum(
            "kw,hwc->hkc", forward_dft, normed, preferred_element_type=jnp.float32
        ).astype(jnp.bfloat16)
        modal_data = to_modes(spectrum)
        coefficients = jnp.einsum(
            "mlh,hmrc->mlrc", analysis, modal_data, preferred_element_type=jnp.float32
        )
        filtered = filter_modes(coefficients, filter_real, filter_imag).astype(jnp.bfloat16)
        synthesized = jnp.einsum(
            "mlh,mlrc->hmrc", synthesis, filtered, preferred_element_type=jnp.float32
        ).astype(jnp.bfloat16)
        banded = to_bands(synthesized)
        mixed_grid = jnp.einsum(
            "wk,hkc->hwc", inverse_dft, banded, preferred_element_type=jnp.float32
        )
        residual = values + mixed_grid
        normed_two = (
            norm_plain(residual, gain_pair[1], bias_pair[1])
            .astype(jnp.bfloat16)
            .reshape(-1, channel_count)
        )
        hidden = jnp.dot(normed_two, weight_in, preferred_element_type=jnp.float32) + shift_in
        active = gelu_tanh(hidden).astype(jnp.bfloat16)
        output = jnp.dot(active, weight_out, preferred_element_type=jnp.float32) + shift_out
        saved_state = (values, coefficients, residual, hidden)
        return (residual + output.reshape(values.shape), saved_state)

    def backward_layer(grad_out, saved_state, params):
        gain_pair, bias_pair, filter_pair, weight_in, shift_in, weight_out, shift_out = params
        filter_real, filter_imag = filter_parts(filter_pair)
        values, coefficients, residual, hidden = saved_state
        normed_two_full, norm_two_pull = jax.vjp(norm_plain, residual, gain_pair[1], bias_pair[1])
        normed_two = normed_two_full.astype(jnp.bfloat16).reshape(-1, channel_count)
        active_full, gelu_pull = jax.vjp(gelu_tanh, hidden)
        active = active_full.astype(jnp.bfloat16)
        flat_grad = grad_out.reshape(-1, channel_count)
        grad_shift_out = jnp.sum(flat_grad, axis=0)
        grad_low = flat_grad.astype(jnp.bfloat16)
        grad_weight_out = jnp.einsum(
            "pf,pc->fc", active, grad_low, preferred_element_type=jnp.float32
        )
        grad_active = jnp.einsum(
            "pc,fc->pf", grad_low, weight_out, preferred_element_type=jnp.float32
        )
        grad_hidden = gelu_pull(grad_active)[0]
        grad_shift_in = jnp.sum(grad_hidden, axis=0)
        hidden_low = grad_hidden.astype(jnp.bfloat16)
        grad_weight_in = jnp.einsum(
            "pc,pf->cf", normed_two, hidden_low, preferred_element_type=jnp.float32
        )
        grad_normed_two = jnp.einsum(
            "pf,cf->pc", hidden_low, weight_in, preferred_element_type=jnp.float32
        )
        grad_norm_res, grad_gain_two, grad_bias_two = norm_two_pull(
            grad_normed_two.reshape(residual.shape)
        )
        grad_residual = grad_out + grad_norm_res
        mixed_low = grad_residual.astype(jnp.bfloat16)
        grad_banded = jnp.einsum(
            "wk,hwc->hkc", inverse_dft, mixed_low, preferred_element_type=jnp.float32
        ).astype(jnp.bfloat16)
        grad_modal = grad_to_modes(grad_banded)
        grad_filtered = jnp.einsum(
            "mlh,hmrc->mlrc", synthesis, grad_modal, preferred_element_type=jnp.float32
        )
        filtered_full, filter_pull = jax.vjp(filter_modes, coefficients, filter_real, filter_imag)
        grad_coefficients, grad_filter_real, grad_filter_imag = filter_pull(grad_filtered)
        grad_spectrum = jnp.einsum(
            "mlh,mlrc->hmrc",
            analysis,
            grad_coefficients.astype(jnp.bfloat16),
            preferred_element_type=jnp.float32,
        ).astype(jnp.bfloat16)
        grad_lat = grad_to_bands(grad_spectrum)
        grad_normed = jnp.einsum(
            "kw,hkc->hwc", forward_dft, grad_lat, preferred_element_type=jnp.float32
        )
        normed_full, norm_one_pull = jax.vjp(first_norm, values, gain_pair[0], bias_pair[0])
        grad_norm_in, grad_gain_one, grad_bias_one = norm_one_pull(grad_normed)
        grad_values = grad_residual + grad_norm_in
        layer_grads = (
            jnp.stack([grad_gain_one, grad_gain_two]),
            jnp.stack([grad_bias_one, grad_bias_two]),
            jnp.stack([grad_filter_real, grad_filter_imag]),
            grad_weight_in,
            grad_shift_in,
            grad_weight_out,
            grad_shift_out,
        )
        return (grad_values, layer_grads)

    gathered = (
        lax.all_gather(norm_gains.astype(jnp.bfloat16), "pipe", axis=0, tiled=True).astype(
            norm_gains.dtype
        ),
        lax.all_gather(norm_biases.astype(jnp.bfloat16), "pipe", axis=0, tiled=True).astype(
            norm_biases.dtype
        ),
        lax.all_gather(filters.astype(jnp.bfloat16), "pipe", axis=0, tiled=True).astype(
            filters.dtype
        ),
        lax.all_gather(
            w_in.astype(jnp.float32).astype(jnp.bfloat16), "pipe", axis=0, tiled=True
        ).astype(jnp.float32),
        lax.all_gather(bias_in.astype(jnp.bfloat16), "pipe", axis=0, tiled=True).astype(
            bias_in.dtype
        ),
        lax.all_gather(
            w_out.astype(jnp.float32).astype(jnp.bfloat16), "pipe", axis=0, tiled=True
        ).astype(jnp.float32),
        lax.all_gather(bias_out.astype(jnp.bfloat16), "pipe", axis=0, tiled=True).astype(
            bias_out.dtype
        ),
    )
    all_gains, all_biases, all_filters, all_win, all_bin, all_wout, all_bout = gathered
    layer_params = [
        (
            all_gains[layer_number],
            all_biases[layer_number],
            all_filters[layer_number],
            all_win[layer_number].astype(jnp.bfloat16),
            all_bin[layer_number],
            all_wout[layer_number].astype(jnp.bfloat16),
            all_bout[layer_number],
        )
        for layer_number in range(2)
    ]
    half_count = micro_count // 2
    sending = jnp.where(section_index == 0, edges[0, half_count:], edges[0, :half_count])
    arrived = swapped(sending, "pipe", 0)
    my_inputs = jnp.where(section_index == 0, edges[0, :half_count], arrived)
    my_cotangents = jnp.where(section_index == 0, arrived, edges[0, half_count:])
    first_out, first_state = forward_layer(my_inputs[0].astype(jnp.float32), layer_params[0])
    second_out, second_state = forward_layer(first_out, layer_params[1])
    output_list = [second_out]
    grad_middle, grads_second = backward_layer(
        my_cotangents[0].astype(jnp.float32), second_state, layer_params[1]
    )
    grad_start, grads_first = backward_layer(grad_middle, first_state, layer_params[0])
    grad_list = [grad_start]
    stacked = tuple(
        (
            jnp.stack([first_entry, second_entry])
            for first_entry, second_entry in zip(grads_first, grads_second)
        )
    )
    mine = (
        lax.psum_scatter(
            stacked[0].astype(jnp.bfloat16), "pipe", scatter_dimension=0, tiled=True
        ).astype(jnp.float32),
        lax.psum_scatter(
            stacked[1].astype(jnp.bfloat16), "pipe", scatter_dimension=0, tiled=True
        ).astype(jnp.float32),
        lax.psum_scatter(
            stacked[2].astype(jnp.bfloat16), "pipe", scatter_dimension=0, tiled=True
        ).astype(jnp.float32),
        lax.psum_scatter(
            stacked[3].astype(jnp.bfloat16), "pipe", scatter_dimension=0, tiled=True
        ).astype(jnp.float32),
        lax.psum_scatter(
            stacked[4].astype(jnp.bfloat16), "pipe", scatter_dimension=0, tiled=True
        ).astype(jnp.float32),
        lax.psum_scatter(
            stacked[5].astype(jnp.bfloat16), "pipe", scatter_dimension=0, tiled=True
        ).astype(jnp.float32),
        lax.psum_scatter(
            stacked[6].astype(jnp.bfloat16), "pipe", scatter_dimension=0, tiled=True
        ).astype(jnp.float32),
    )
    totals = tuple((entry[0] for entry in mine))
    output_half = jnp.stack(output_list)
    grad_half = jnp.stack(grad_list)
    reply = jnp.where(section_index == 0, output_half, grad_half)
    returned = swapped(for_sending(reply), "pipe", 0).astype(reply.dtype)
    ends = jnp.where(
        section_index == 0,
        jnp.concatenate([grad_half, returned], axis=0),
        jnp.concatenate([returned, output_half], axis=0),
    )[None]
    gain_grads, bias_grads, filter_grads, win_grads, bin_grads, wout_grads, bout_grads = totals
    gain_part, bias_part, filter_part, win_part, bin_part, wout_part, bout_part = (
        lax.psum_scatter(
            gain_grads.astype(jnp.bfloat16), "space", scatter_dimension=1, tiled=True
        ).astype(jnp.float32),
        lax.psum_scatter(
            bias_grads.astype(jnp.bfloat16), "space", scatter_dimension=1, tiled=True
        ).astype(jnp.float32),
        lax.psum_scatter(
            filter_grads.astype(jnp.bfloat16), "space", scatter_dimension=2, tiled=True
        ).astype(jnp.float32),
        lax.psum_scatter(
            win_grads.astype(jnp.bfloat16), "space", scatter_dimension=0, tiled=True
        ).astype(jnp.float32),
        lax.psum_scatter(
            bin_grads.astype(jnp.bfloat16), "space", scatter_dimension=0, tiled=True
        ).astype(jnp.float32),
        lax.psum_scatter(
            wout_grads.astype(jnp.bfloat16), "space", scatter_dimension=0, tiled=True
        ).astype(jnp.float32),
        lax.psum_scatter(
            bout_grads.astype(jnp.bfloat16), "space", scatter_dimension=0, tiled=True
        ).astype(jnp.float32),
    )
    summed = (
        lax.psum(gain_part.astype(jnp.bfloat16), "dp").astype(jnp.float32),
        lax.psum(bias_part.astype(jnp.bfloat16), "dp").astype(jnp.float32),
        lax.psum(filter_part.astype(jnp.bfloat16), "dp").astype(jnp.float32),
        lax.psum(win_part.astype(jnp.bfloat16), "dp").astype(jnp.float32),
        lax.psum(bin_part.astype(jnp.bfloat16), "dp").astype(jnp.float32),
        lax.psum(wout_part.astype(jnp.bfloat16), "dp").astype(jnp.float32),
        lax.psum(bout_part.astype(jnp.bfloat16), "dp").astype(jnp.float32),
    )
    return (ends,) + tuple((entry[None] for entry in summed))


def local(edges, mask_levels, norm_gains, norm_biases, filters, w_in, bias_in, w_out, bias_out):
    bands = lax.axis_size("space")
    lat, lon, ch = edges.shape[2:]
    odd = lat % ROWS or lat % bands or lon != 2 * lat * bands or bands != 4
    if odd or edges.shape[1] != 2:
        return plain_local(
            edges, mask_levels, norm_gains, norm_biases, filters, w_in, bias_in, w_out, bias_out
        )
    ff = w_in.shape[2]
    orders = lon // 2
    own = orders // bands
    degrees = lat * bands
    sub = 2
    group = 4
    points = lat * lon
    high_count = lat // bands
    low_count = own - high_count
    d = Dims(
        bands, lat, lon, ch, own, degrees, ff, ROWS, lat // ROWS, sub, ROWS // sub, group,
        low_count, high_count,
    )
    core = lax.axis_index("pipe")
    space = lax.axis_index("space")
    edges = edges.reshape(1, 2, points, ch)
    mask = mask_levels.reshape(points, ch)

    low_orders = space + bands * jnp.arange(-(-low_count // 8) * 8, dtype=jnp.int32)
    step = jnp.arange(bands * high_count, dtype=jnp.int32)
    high_orders = bands * (low_count + step % high_count) + step // high_count
    own_weights = (
        norm_gains, norm_biases, filters, w_in, bias_in[:, None, :], w_out, bias_out[:, None, :],
    )
    orders_in = legendre_orders(jnp.concatenate([low_orders, high_orders]))
    x0, level, *made = point_start_call(d, edges, mask, own_weights, orders_in)
    analysis, synthesis, high_analysis, high_synthesis = made[:4]
    forward, forward_t, inverse, inverse_t, arrived = made[4:9]
    gains, biases, filt, win, bin_, wout, bout, *sent = made[9:]

    grid_f32 = (jax.ShapeDtypeStruct((points, ch), F32), sub_spec(d, ch))
    small = lambda *arrays: [(a, None) for a in arrays]
    grid = lambda *arrays: [(a, sub_spec(d, ch)) for a in arrays]
    levels = [(level, sub_spec(d, 128))]
    table = lambda a, b: jax.ShapeDtypeStruct((a, b), F32)
    sums = lambda *widths: [(sum_shape(d, w), None) for w in widths]
    low = step_scratch(d, ch, BF)
    acc = step_scratch(d, ch, F32)
    hid = step_scratch(d, ff, F32)
    act = step_scratch(d, ff, BF)
    stat = step_scratch(d, 128, F32)
    dft = 2 * orders * ch
    ffn = ch * ff
    tables = (analysis, synthesis, filt)
    weight_grads = [(table(ch, ff), None), (sum_shape(d, ff), None), (table(ff, ch), None)]
    coefficients = [
        (jax.ShapeDtypeStruct((low_count, degrees, 2 * ch), F32), coefficient_spec(d)),
        (jax.ShapeDtypeStruct((high_total(d), ch), F32), None),
    ]
    filter_grad = (jax.ShapeDtypeStruct((2, degrees, ch), F32), None)

    *coef0, res0, x1, sent, sent_high = fused_call(
        d, (spectral, point_middle), "spectral_first_point_middle", 3,
        order_specs(d, 0, sent, tables), (high_synthesis, high_analysis),
        grid(x0) + levels + small(gains, biases, win, bin_, wout, bout, inverse, forward),
        coefficients, [grid_f32, grid_f32],
        [low, acc, hid, act, stat, stat, stat], (), point_cost(d, 2 * dft + 2 * ffn, 18),
    )
    held_shape = jax.ShapeDtypeStruct((2, points, ch), BF)
    (
        *coef1, held, d_res1, g_win1, g_bin1, g_wout1, g_bout1, g_gain21, g_bias21, sent,
        sent_high,
    ) = fused_call(
        d, (spectral, point_turn), "spectral_second_point_turn", 4,
        order_specs(d, 1, (sent, sent_high), tables), (high_synthesis, high_synthesis),
        grid(x1) + [(edges[0], half_spec(d, 1))] + grid(arrived)
        + small(gains, biases, win, bin_, wout, bout, inverse, inverse_t),
        coefficients,
        [(held_shape, half_spec(d, 1)), grid_f32] + weight_grads + sums(ch, ch, ch),
        [low, low, acc, acc, hid, hid, act, act, stat, stat, stat, stat],
        (4, 5, 6, 7, 8, 9), point_cost(d, 2 * dft + 6 * ffn, 20),
    )
    (
        g_filt1, d_res0, g_win0, g_bin0, g_wout0, g_bout0, g_gain20, g_bias20, g_gain11, g_bias11,
        sent, sent_high,
    ) = fused_call(
        d, (spectral_back, point_back), "spectral_back_point_back", 5,
        order_specs(d, 1, (sent, sent_high), tables, coef1), (high_analysis, high_synthesis),
        grid(x1) + levels + grid(d_res1, res0)
        + small(gains, biases, win, bin_, wout, forward_t, inverse_t),
        [filter_grad], [grid_f32] + weight_grads + sums(ch, ch, ch, ch, ch),
        [low, low, acc, hid, hid, act, act, stat, stat, stat, stat],
        (0, 2, 3, 4, 5, 6, 7, 8, 9), point_cost(d, 2 * dft + 5 * ffn, 24),
    )
    grads = (
        g_win0, g_bin0, g_wout0, g_bout0, g_gain20, g_bias20,
        g_win1, g_bin1, g_wout1, g_bout1, g_gain21, g_bias21, g_filt1, g_gain11, g_bias11,
    )
    pairs, groups = lax.axis_size("pipe"), lax.axis_size("dp")
    held, result, rest, returned = end_call(
        d, pairs, groups, order_specs(d, 0, (sent, sent_high), tables, coef0),
        grid(x0) + levels + grid(d_res0), (gains, forward_t, high_analysis), grads, held
    )
    ends, *small_grads = place_call(d, core, space, held, returned, result, rest, 4 * lon)
    small_grads[2] = jnp.swapaxes(small_grads[2], 2, 3)
    return (ends.reshape(1, 2, lat, lon, ch), *small_grads)


def solution(mesh):
    return jax.shard_map(
        local,
        mesh=mesh,
        in_specs=(
            P("pipe", "dp", "space", None, None),
            P("space", None, None),
            P("pipe", None, None),
            P("pipe", None, None),
            P("pipe", None, None, None),
            P("pipe", None, None),
            P("pipe", None),
            P("pipe", None, None),
            P("pipe", None),
        ),
        out_specs=(
            P("pipe", "dp", "space", None, None),
            P("pipe", None, "space"),
            P("pipe", None, "space"),
            P("pipe", None, None, "space"),
            P("pipe", "space", None),
            P("pipe", "space"),
            P("pipe", "space", None),
            P("pipe", "space"),
        ),
        check_vma=False,
    )
```
